32 devices in a mesh: fsdp: 2 (over x), ctx: 4 (over z), tp: 4 (over y, core).
Axes of the slice: x: 2, y: 2, z: 4, core: 2. Of those that a mesh axis runs over, the one named last changes fastest.
Arguments:
- hidden: bfloat16 [4, 1024, 1024], P('fsdp', 'ctx'), may hold values from -6 to 6
- lengths: int32 [4], P('fsdp'), may hold values from 128 to 1024, as said below
- w_qkv: bfloat16 [1024, 3, 1024], P('fsdp', None, 'tp'), may hold values from -0.1875 to 0.1875
- b_qkv: bfloat16 [2, 4, 256], P(None, 'tp', 'fsdp'), may hold values from -3 to 3
- w_out: bfloat16 [1024, 1024], P('tp', 'fsdp'), may hold values from -0.5 to 0.5
- norm_gain: bfloat16 [2, 1024], P(None, 'fsdp'), may hold values from 0.25 to 1.75
- shifts: bfloat16 [4, 1024], P(None, 'fsdp'), may hold values from -2 to 2
- up_weight: bfloat16 [1024, 4096], P('fsdp', 'tp'), may hold values from -0.1875 to 0.1875
- b_up: bfloat16 [4, 1024], P('tp', 'fsdp'), may hold values from -3 to 3
- down_weight: bfloat16 [4096, 1024], P('tp', 'fsdp'), may hold values from -0.09375 to 0.09375
- cotangent: bfloat16 [4, 1024, 1024], P('fsdp', 'ctx'), may hold values from -6 to 6
Outputs:
- out: bfloat16 [4, 1024, 1024], P('fsdp', 'ctx')
- grad_hidden: bfloat16 [4, 1024, 1024], P('fsdp', 'ctx')
- grad_w_qkv: float32 [1024, 3, 1024], P('fsdp', None, 'tp')
- grad_b_qkv: float32 [2, 4, 256], P(None, 'tp', 'fsdp')
- grad_w_out: float32 [1024, 1024], P('tp', 'fsdp')
- grad_norm_gain: float32 [2, 1024], P(None, 'fsdp')
- grad_shifts: float32 [4, 1024], P(None, 'fsdp')
- grad_w_up: float32 [1024, 4096], P('fsdp', 'tp')
- grad_b_up: float32 [4, 1024], P('tp', 'fsdp')
- grad_w_down: float32 [4096, 1024], P('tp', 'fsdp')
The draws below stay inside these ranges and needn't reach their ends.
Inputs may be any that keep to these rules, and one draw needn't show every extreme that they name: `lengths`: in each group of 2 slots that share an index of fsdp, one slot, chosen by the seed, holds all 1024 tokens. A slot's tokens are its first positions; the rest are padding.
All inputs are finite; a program needn't handle non-finite values.
Results may differ from the reference program's by a relative error of at most 0.022.
The reference program's roundings to bfloat16 on the way count: a program that leaves them out, or rounds other values in their place, can miss the bound.
Values may be sent and summed in bfloat16 or wider, within the bound.
No kernel may reach another device: no remote copies, remote signals or barrier semaphores. Data moves between devices by JAX's collectives and lax.ppermute only.
A program may use at most 128 MiB of HBM per device.

```python
import jax
import jax.numpy as jnp
from jax import lax

MODEL_WIDTH = 1024
H = 16
HD = 64
FF = 4096
LEN = 1024
SEQS = 2
SEQUENCES = 4
N_TP = 4


def draw_lengths(key, part):
    key = jax.random.fold_in(key, 7)
    key_one, key_two = jax.random.split(key)
    groups = SEQUENCES // SEQS
    picked = jax.random.randint(key_one, (groups, SEQS), LEN // 8, LEN + 1)
    chosen = jax.random.randint(key_two, (groups, 1), 0, SEQS)
    places = jnp.arange(SEQS, dtype=jnp.int32)[None, :]
    return jnp.where(places == chosen, LEN, picked).reshape(SEQUENCES).astype(jnp.int32)


def strengthened(drawn, stream_key, source, target, parts, factor):
    def block_of(dim):
        return (jnp.arange(drawn.shape[dim]) // (drawn.shape[dim] // parts)).reshape((-1,) + (1,) * (drawn.ndim - 1 - dim))

    first = jax.random.permutation(stream_key, parts)[block_of(target)]
    second = (block_of(target) + parts // 2) % parts
    return jnp.where((block_of(source) == first) | (block_of(source) == second), factor * drawn, drawn)


def levels(stream_key, shape, cuts, least, top_value):
    def one(position, shards_of):
        draws = jax.random.uniform(jax.random.fold_in(jax.random.fold_in(stream_key, 6), position), (shards_of,), jnp.float32, least / len(cuts), top_value / len(cuts))
        return jnp.repeat(jnp.exp(draws), shape[position] // shards_of).reshape((-1,) + (1,) * (len(shape) - position - 1))

    level = one(*cuts[0])
    for cut in cuts[1:]:
        level = level * one(*cut)
    return level


def normal_values(key, shape, scale, limit, cuts=(), held_as=jnp.bfloat16):
    level = levels(key, shape, cuts, -0.22, 0.18) if cuts else 1.0
    array = jax.random.normal(key, shape, jnp.float32) * scale * level
    return jnp.minimum(jnp.maximum(array, -limit), limit).astype(held_as)


def heavy_noise(own_key, extent, spread, bound, cuts, heavy, kind=jnp.bfloat16):
    entries = spread * jax.random.normal(own_key, extent, jnp.float32)
    if cuts:
        entries = entries * levels(own_key, extent, cuts, -0.22, 0.18)
    return jnp.clip(strengthened(entries, jax.random.fold_in(own_key, 3), *heavy), -bound, bound).astype(kind)


def setup_inputs(seed: int = 0) -> dict:
    key_list = jax.random.split(jax.random.key(seed), 12)
    return {
        "hidden": heavy_noise(key_list[0], (SEQUENCES, LEN, MODEL_WIDTH), 1.0, 6.0, ((0, 2), (1, 4)), (0, 2, 2, 2.0)),
        "lengths": draw_lengths(jax.random.fold_in(key_list[11], 71), 0),
        "w_qkv": normal_values(key_list[2], (MODEL_WIDTH, 3, MODEL_WIDTH), MODEL_WIDTH ** -0.5, 0.1875, ((0, 2), (2, 4))),
        "b_qkv": normal_values(key_list[3], (2, N_TP, MODEL_WIDTH // N_TP), 0.5, 3.0, ((1, 4), (2, 2))),
        "w_out": normal_values(key_list[4], (MODEL_WIDTH, MODEL_WIDTH), (MODEL_WIDTH // 8) ** -0.5, 0.5, ((0, 4), (1, 2))),
        "norm_gain": jnp.clip(1.0 + 0.15 * jax.random.normal(key_list[5], (2, MODEL_WIDTH), jnp.float32), 0.25, 1.75).astype(jnp.bfloat16),
        "shifts": normal_values(key_list[6], (4, MODEL_WIDTH), 0.3, 2.0, ((1, 2),)),
        "up_weight": normal_values(key_list[7], (MODEL_WIDTH, FF), MODEL_WIDTH ** -0.5, 0.1875, ((0, 2), (1, 4))),
        "b_up": normal_values(key_list[8], (N_TP, FF // N_TP), 0.5, 3.0, ((0, 4), (1, 2))),
        "down_weight": normal_values(key_list[9], (FF, MODEL_WIDTH), FF ** -0.5, 0.09375, ((0, 4), (1, 2))),
        "cotangent": heavy_noise(key_list[10], (SEQUENCES, LEN, MODEL_WIDTH), 1.0, 6.0, ((0, 2), (1, 4)), (0, 2, 2, 2.0)),
    }


EPSILON = 1e-12
NEGATIVE = -1e+30
HIGH_PRECISION = lax.Precision.HIGHEST

@jax.custom_vjp
def low(v):
    return lax.optimization_barrier(v.astype(jnp.bfloat16)).astype(jnp.float32)

@jax.custom_vjp
def low_back(v):
    return v

def low_keep(v):
    return (low(v), None)

def low_pass(kept, grad):
    return (grad,)

def back_keep(v):
    return (v, None)

def back_low(kept, grad):
    return (low(grad),)
low.defvjp(low_keep, low_pass)
low_back.defvjp(back_keep, back_low)

def layer_norm(values):
    centre = lax.optimization_barrier(jnp.mean(values, axis=-1, keepdims=True))
    shifted = values - centre
    return shifted * lax.rsqrt(lax.optimization_barrier(jnp.mean(shifted * shifted, axis=-1, keepdims=True)) + EPSILON)

def gelu_exact(values):
    return 0.5 * values * (1.0 + lax.erf(values * 0.7071067811865476))

def attend_sequence(packed):
    triple, valid = packed
    scores = jnp.einsum('qhd,khd->hqk', triple[0], triple[1], precision=HIGH_PRECISION) * HD ** (-0.5)
    scores = low_back(scores)
    masked = jnp.where(valid[None, None, :], scores, NEGATIVE)
    peak = lax.optimization_barrier(jnp.max(masked, axis=-1, keepdims=True))
    weights = jnp.exp(masked - peak)
    probs = weights / lax.optimization_barrier(jnp.sum(weights, axis=-1, keepdims=True))
    return jnp.einsum('hqk,khd->qhd', low(probs), triple[2], precision=HIGH_PRECISION)

def group_forward(tokens, lens, params):
    w_qkv, b_qkv, w_out, gains, shifts, up_weight, b_up, down_weight = params
    row_count = SEQS * LEN
    shard = MODEL_WIDTH // N_TP
    unit_vector = FF // N_TP
    rows = tokens.reshape(row_count, MODEL_WIDTH)
    wide = low_back(jnp.broadcast_to(rows, (N_TP, row_count, MODEL_WIDTH)))
    proj = jnp.einsum('trd,dkte->ktre', wide, w_qkv.reshape(MODEL_WIDTH, 3, N_TP, shard), precision=HIGH_PRECISION)
    biases = b_qkv.reshape(2, N_TP, 1, shard)
    triple = jnp.stack([proj[0] + biases[0], proj[1], proj[2] + biases[1]])
    triple = low(low_back(triple))
    heads = triple.reshape(3, N_TP, SEQS, LEN, H // N_TP, HD).transpose(2, 0, 3, 1, 4, 5)
    heads = heads.reshape(SEQS, 3, LEN, H, HD)
    valid = jnp.arange(LEN, dtype=jnp.int32)[None, :] < lens[:, None]
    attn = lax.map(jax.checkpoint(attend_sequence), (heads, valid))
    attn = low(low_back(attn.reshape(row_count, N_TP, shard)))
    partial_one = jnp.einsum('rtc,tcd->trd', attn, w_out.reshape(N_TP, shard, MODEL_WIDTH), precision=HIGH_PRECISION)
    branch = low_back(lax.optimization_barrier(jnp.sum(low(partial_one), axis=0))) + shifts[0]
    mid = layer_norm(rows + branch) * gains[0] + shifts[1]
    middle_broad = low_back(jnp.broadcast_to(low(mid), (N_TP, row_count, MODEL_WIDTH)))
    preactivation = jnp.einsum('uaq,qup->uap', middle_broad, up_weight.reshape(MODEL_WIDTH, N_TP, unit_vector), precision=HIGH_PRECISION)
    preactivation = low_back(preactivation + b_up.reshape(N_TP, 1, unit_vector))
    activation = low(gelu_exact(preactivation))
    second_partial = jnp.einsum('pev,pvl->pel', activation, down_weight.reshape(N_TP, unit_vector, MODEL_WIDTH), precision=HIGH_PRECISION)
    branch_two = low_back(lax.optimization_barrier(jnp.sum(low(second_partial), axis=0))) + shifts[2]
    final = layer_norm(mid + branch_two) * gains[1] + shifts[3]
    return final.reshape(SEQS, LEN, MODEL_WIDTH)

def reference(hidden, lengths, w_qkv, b_qkv, w_out, norm_gain, shifts, up_weight, b_up, down_weight, cotangent):
    groups = hidden.shape[0] // SEQS
    params = tuple((item.astype(jnp.float32) for item in (w_qkv, b_qkv, w_out, norm_gain, shifts, up_weight, b_up, down_weight)))
    lens = lengths.reshape(groups, SEQS)

    def forward(tokens, weights):

        def one_group(packed):
            return group_forward(packed[0], packed[1], weights)
        stacked = tokens.reshape(groups, SEQS, LEN, MODEL_WIDTH)
        return lax.map(jax.checkpoint(one_group), (stacked, lens)).reshape(hidden.shape)
    final, pullback = jax.vjp(forward, hidden.astype(jnp.float32), params)
    grad_tokens, grads = pullback(cotangent.astype(jnp.float32))
    return (final.astype(jnp.bfloat16), grad_tokens.astype(jnp.bfloat16), grads[0], grads[1], grads[2], grads[3], grads[4], grads[5], grads[6], grads[7])
```

```python
import functools

import jax
import jax.numpy as jnp
from jax import lax
from jax.experimental import pallas as pl
from jax.experimental.pallas import tpu as pltpu
from jax.sharding import PartitionSpec as P

HD = 64
EPSILON = 1e-12
NEGATIVE = -1e30
F32 = jnp.float32
BF16 = jnp.bfloat16
VMEM_LIMIT = 48 * 1024 * 1024

NT = (((1,), (1,)), ((), ()))
TN = (((0,), (0,)), ((), ()))
NN = (((1,), (0,)), ((), ()))


def mm(a, b, dims=NN):
    return lax.dot_general(a, b, dims, preferred_element_type=F32)


def swap_core(value):
    n = lax.axis_size("tp")
    return lax.ppermute(value, "tp", [(i, i ^ 1) for i in range(n)])


def swap_y(value):
    n = lax.axis_size("tp")
    return lax.ppermute(value, "tp", [(i, i ^ 2) for i in range(n)])


def gather_parts(value):
    n = lax.axis_size("fsdp")
    parts = [value]
    for d in range(1, n):
        parts.append(lax.ppermute(value, "fsdp", [((i + d) % n, i) for i in range(n)]))
    return parts


def few(parts, axis):
    return parts if len(parts) == 2 else [jnp.concatenate(parts, axis=axis)]


def grad_blocks(left, right, n, axis):
    if n == 2:
        size = (left, right)[axis].shape[1] // n
        cut = [slice(d * size, (d + 1) * size) for d in range(n)]
        blocks = [
            mm(left[:, c], right, TN) if axis == 0 else mm(left, right[:, c], TN) for c in cut
        ]
    else:
        blocks = jnp.split(mm(left, right, TN), n, axis=axis)
    return blocks[:1] + [b.astype(BF16) for b in blocks[1:]]


def scatter_sum(blocks):
    n = lax.axis_size("fsdp")
    total = blocks[0]
    for d in range(1, n):
        total = total + lax.ppermute(
            blocks[d], "fsdp", [(i, (i + d) % n) for i in range(n)]
        ).astype(F32)
    return total


def ctx_sum(value):
    n = lax.axis_size("ctx")
    if n != 4:
        return lax.psum(value, "ctx")
    place = lax.axis_index("ctx")
    middle = (place == 1) | (place == 2)
    kind = value.dtype
    first = lax.ppermute(value, "ctx", [(0, 1), (3, 2)])
    pair = (value.astype(F32) + first.astype(F32)).astype(kind)
    second = lax.ppermute(pair, "ctx", [(1, 2), (2, 1)])
    total = (pair.astype(F32) + second.astype(F32)).astype(kind)
    third = lax.ppermute(total, "ctx", [(1, 0), (2, 3)])
    return jnp.where(middle, total, third)


def tp_sum_own(partial):
    rows = partial.shape[0] // 2
    other = swap_core(partial[rows:])
    pair = (partial[:rows].astype(F32) + other.astype(F32)).astype(BF16)
    return pair.astype(F32) + swap_y(pair).astype(F32)


def share_core(own):
    return jnp.concatenate([own, swap_core(own)], axis=0)


def turn(value, axis, shift):
    size = value.shape[axis]
    doubled = jnp.concatenate([value, value], axis=axis)
    return lax.dynamic_slice_in_dim(doubled, shift, size, axis=axis)


def call(kernel, out_shape, scratch=(), flops=0, n_bytes=0, trans=0, smem=0, n_in=1):
    specs = [pl.BlockSpec(memory_space=pltpu.SMEM)] * smem + [
        pl.BlockSpec(memory_space=pltpu.VMEM)
    ] * (n_in - smem)
    outs = jax.tree.map(lambda _: pl.BlockSpec(memory_space=pltpu.VMEM), out_shape)
    return pl.pallas_call(
        kernel,
        out_shape=out_shape,
        in_specs=specs,
        out_specs=outs,
        scratch_shapes=list(scratch),
        compiler_params=pltpu.CompilerParams(vmem_limit_bytes=VMEM_LIMIT),
        cost_estimate=pl.CostEstimate(flops=flops, bytes_accessed=n_bytes, transcendentals=trans),
    )


def lane_low(rows):
    return lax.broadcasted_iota(jnp.int32, (rows, 2 * HD), 1) < HD


def pack_heads(rows_value, out_ref, base, length):
    low = lane_low(length)
    for tile in range(rows_value.shape[1] // (2 * HD)):
        a = rows_value[:length, tile * 128 : tile * 128 + 128]
        b = rows_value[length:, tile * 128 : tile * 128 + 128]
        even = jnp.where(low, a, pltpu.roll(b, HD, 1))
        odd = jnp.where(low, pltpu.roll(a, HD, 1), b)
        out_ref[2 * tile, base : base + length, :] = even.astype(BF16)
        out_ref[2 * tile + 1, base : base + length, :] = odd.astype(BF16)


def unpack_heads(in_ref, base, length, tile):
    low = lane_low(length)
    even = in_ref[2 * tile, base : base + length, :].astype(F32)
    odd = in_ref[2 * tile + 1, base : base + length, :].astype(F32)
    a = jnp.where(low, even, pltpu.roll(odd, HD, 1))
    b = jnp.where(low, pltpu.roll(even, HD, 1), odd)
    return a, b


def project_kernel(n_parts, length, *refs):
    x_ref = refs[0]
    bias_ref = refs[1]
    w_refs = refs[2 : 2 + n_parts]
    out_ref = refs[2 + n_parts]
    block = w_refs[0].shape[0]
    acc = mm(x_ref[:, :block], w_refs[0][...])
    for d in range(1, n_parts):
        acc += mm(x_ref[:, d * block : (d + 1) * block], w_refs[d][...])
    acc += bias_ref[...]
    pack_heads(acc, out_ref, 0, length)


def project(x, bias, parts, length):
    rows, width = x.shape
    cols = parts[0].shape[1]
    kernel = functools.partial(project_kernel, len(parts), length)
    return call(
        kernel,
        jax.ShapeDtypeStruct((cols // HD, length, 2 * HD), BF16),
        flops=2 * rows * width * cols,
        n_bytes=2 * (rows * width + width * cols + rows * cols),
        n_in=2 + len(parts),
    )(x, bias, *parts)


def masked_sides(scal_ref, slot, q, k):
    rows = q.shape[0]
    keys = k.shape[0]
    lane_q = lax.broadcasted_iota(jnp.int32, (rows, 2 * HD), 1)
    lane_k = lax.broadcasted_iota(jnp.int32, (keys, 2 * HD), 1)
    spare = HD * (1 - slot)
    mine_q = (lane_q >= slot * HD) & (lane_q < slot * HD + HD)
    q_side = jnp.where(mine_q, q.astype(F32) * (HD ** -0.5), 0.0)
    q_side = jnp.where(lane_q == spare, 1.0, q_side).astype(BF16)
    place = lax.broadcasted_iota(jnp.int32, (keys, 2 * HD), 0) ^ scal_ref[2]
    bias = jnp.where(place < scal_ref[slot], 0.0, NEGATIVE)
    k_side = jnp.where(lane_k == spare, bias, k.astype(F32)).astype(BF16)
    return q_side, k_side


def attend_kernel(block, scal_ref, q_ref, k_ref, v_ref, out_ref, lse_ref):
    length = q_ref.shape[0]
    v_t = v_ref[...].astype(F32).T.astype(BF16)
    k_val = k_ref[...]
    sides = [masked_sides(scal_ref, s, q_ref[...], k_val) for s in range(2)]
    low = lax.broadcasted_iota(jnp.int32, (2 * HD, block), 0) < HD
    for start in range(0, length, block):
        results = []
        for s in range(2):
            q_side, k_side = sides[s]
            scores = mm(k_side, q_side[start : start + block], NT)
            peak = jnp.max(scores, axis=0, keepdims=True)
            weights = jnp.exp(scores - peak)
            total = jnp.sum(weights, axis=0, keepdims=True)
            res = mm(v_t, weights.astype(BF16))
            results.append(res * (1.0 / total))
            lse_ref[s : s + 1, start : start + block] = peak + jnp.log(total)
        both = jnp.where(low, results[0], results[1])
        out_ref[start : start + block, :] = both.T.astype(BF16)


def attend(scal, q, k, v):
    length = q.shape[0]
    return call(
        functools.partial(attend_kernel, min(256, length)),
        (
            jax.ShapeDtypeStruct((length, 2 * HD), BF16),
            jax.ShapeDtypeStruct((2, length), F32),
        ),
        flops=8 * length * length * 2 * HD,
        n_bytes=8 * length * 2 * HD,
        trans=2 * length * length,
        smem=1,
        n_in=4,
    )(scal, q, k, v)


def attend_back_kernel(
    block, scal_ref, q_ref, k_ref, v_ref, lse_ref, g_ref, dq_ref, dk_ref, dv_ref, p_ref, s_ref
):
    length = q_ref.shape[0]
    scale = HD ** -0.5
    k_val = k_ref[...]
    v_val = v_ref[...]
    g_val = g_ref[...]
    k_t = k_val.astype(F32).T.astype(BF16)
    lane = lax.broadcasted_iota(jnp.int32, (length, 2 * HD), 1)
    low_t = lax.broadcasted_iota(jnp.int32, (2 * HD, block), 0) < HD
    low = lane < HD
    keep_q = []
    keep_k = []
    keep_v = []
    for s in range(2):
        q_side, k_side = masked_sides(scal_ref, s, q_ref[...], k_val)
        mine = low if s == 0 else ~low
        g_side = jnp.where(mine, g_val.astype(F32), 0.0).astype(BF16)
        grads_q = []
        for start in range(0, length, block):
            scores = mm(k_side, q_side[start : start + block], NT)
            probs = jnp.exp(scores - lse_ref[s : s + 1, start : start + block])
            grad_probs = mm(v_val, g_side[start : start + block], NT)
            delta = jnp.sum(grad_probs * probs, axis=0, keepdims=True)
            grad_scores = (probs * (grad_probs - delta)).astype(BF16)
            p_ref[:, start : start + block] = probs.astype(BF16)
            s_ref[:, start : start + block] = grad_scores
            grads_q.append(mm(k_t, grad_scores))
        keep_q.append(grads_q)
        keep_v.append(mm(p_ref[...], g_val))
        keep_k.append(mm(s_ref[...], q_ref[...]))
    for i, start in enumerate(range(0, length, block)):
        both = jnp.where(low_t, keep_q[0][i], keep_q[1][i]) * scale
        dq_ref[start : start + block, :] = both.T.astype(BF16)
    dk_ref[...] = (jnp.where(low, keep_k[0], keep_k[1]) * scale).astype(BF16)
    dv_ref[...] = jnp.where(low, keep_v[0], keep_v[1]).astype(BF16)


def attend_back(scal, q, k, v, lse, grad):
    length = q.shape[0]
    shape = jax.ShapeDtypeStruct((length, 2 * HD), BF16)
    return call(
        functools.partial(attend_back_kernel, min(256, length)),
        (shape, shape, shape),
        scratch=[pltpu.VMEM((length, length), BF16), pltpu.VMEM((length, length), BF16)],
        flops=20 * length * length * 2 * HD,
        n_bytes=16 * length * 2 * HD,
        trans=2 * length * length,
        smem=1,
        n_in=6,
    )(scal, q, k, v, lse, grad)


def outproj_kernel(n_parts, length, *refs):
    heads_ref = refs[0]
    w_refs = refs[1 : 1 + n_parts]
    attn_ref, part_ref = refs[1 + n_parts :]
    half = length // 2
    for tile in range(heads_ref.shape[0] // 2):
        for s, value in enumerate(unpack_heads(heads_ref, 0, length, tile)):
            for h in range(2):
                at = h * length + s * half
                attn_ref[at : at + half, tile * 128 : tile * 128 + 128] = value[
                    h * half : (h + 1) * half
                ].astype(BF16)
    block = w_refs[0].shape[1]
    for d in range(n_parts):
        part_ref[:, d * block : (d + 1) * block] = mm(attn_ref[...], w_refs[d][...]).astype(BF16)


def outproj(heads, parts):
    n_heads, length, _ = heads.shape
    rows, cols = 2 * length, n_heads * HD
    width = parts[0].shape[1] * len(parts)
    return call(
        functools.partial(outproj_kernel, len(parts), length),
        (
            jax.ShapeDtypeStruct((rows, cols), BF16),
            jax.ShapeDtypeStruct((rows, width), BF16),
        ),
        flops=2 * rows * cols * width,
        n_bytes=2 * (2 * rows * cols + cols * width + rows * width),
        n_in=1 + len(parts),
    )(heads, *parts)


def grad_attn_kernel(n_parts, length, *refs):
    g_ref = refs[0]
    w_refs = refs[1 : 1 + n_parts]
    out_ref = refs[1 + n_parts]
    half = length // 2
    block = w_refs[0].shape[1]
    acc = mm(g_ref[:, :block], w_refs[0][...], NT)
    for d in range(1, n_parts):
        acc += mm(g_ref[:, d * block : (d + 1) * block], w_refs[d][...], NT)
    for h in range(2):
        pack_heads(acc[h * length : (h + 1) * length], out_ref, h * half, half)


def grad_attn(g, parts, length):
    rows, width = g.shape
    cols = parts[0].shape[0]
    return call(
        functools.partial(grad_attn_kernel, len(parts), length),
        jax.ShapeDtypeStruct((cols // HD, length, 2 * HD), BF16),
        flops=2 * rows * width * cols,
        n_bytes=2 * (rows * width + width * cols + rows * cols),
        n_in=1 + len(parts),
    )(g, *parts)


def grad_token_kernel(n_parts, length, *refs):
    d_ref = refs[0]
    w_refs = refs[1 : 1 + 3 * n_parts]
    rows_ref, part_ref = refs[1 + 3 * n_parts :]
    half = length // 2
    cols = d_ref.shape[0] * HD
    for kind in range(3):
        for tile in range(d_ref.shape[0] // 2):
            for s, value in enumerate(unpack_heads(d_ref, kind * length, length, tile)):
                for h in range(2):
                    at = h * length + s * half
                    lane = kind * cols + tile * 128
                    rows_ref[at : at + half, lane : lane + 128] = value[
                        h * half : (h + 1) * half
                    ].astype(BF16)
    block = w_refs[0].shape[0]
    for d in range(n_parts):
        acc = mm(rows_ref[:, :cols], w_refs[d][...], NT)
        for kind in range(1, 3):
            acc += mm(
                rows_ref[:, kind * cols : (kind + 1) * cols], w_refs[kind * n_parts + d][...], NT
            )
        part_ref[:, d * block : (d + 1) * block] = acc.astype(BF16)


def grad_token(heads, parts, length):
    n_heads = heads.shape[0]
    rows, cols = 2 * length, 3 * n_heads * HD
    n_parts = len(parts[0])
    width = parts[0][0].shape[0] * n_parts
    flat = [w for kind in parts for w in kind]
    return call(
        functools.partial(grad_token_kernel, n_parts, length),
        (
            jax.ShapeDtypeStruct((rows, cols), BF16),
            jax.ShapeDtypeStruct((rows, width), BF16),
        ),
        flops=2 * rows * cols * width,
        n_bytes=2 * (2 * rows * cols + cols * width + rows * width),
        n_in=1 + len(flat),
    )(heads, *flat)


def layer_stats(values):
    centre = jnp.mean(values, axis=-1, keepdims=True)
    shifted = values - centre
    inverse = lax.rsqrt(jnp.mean(shifted * shifted, axis=-1, keepdims=True) + EPSILON)
    return (shifted * inverse, inverse)


def norm_back(grad_norm, normed, inverse, gain_row):
    scaled = grad_norm * gain_row
    centre = jnp.mean(scaled, axis=-1, keepdims=True)
    along = jnp.mean(scaled * normed, axis=-1, keepdims=True)
    return inverse * (scaled - centre - normed * along)


def gelu_value(values):
    return 0.5 * values * (1.0 + lax.erf(values * 0.7071067811865476))


def gelu_slope(values):
    return (
        0.5 * (1.0 + lax.erf(values * 0.7071067811865476))
        + values * jnp.exp(-0.5 * values * values) * 0.3989422804014327
    )


def heads_swap(value):
    return lax.all_to_all(value, "ctx", split_axis=0, concat_axis=0, tiled=True)


def on_device(
    hidden, lengths, w_qkv, b_qkv, w_out, norm_gain, shifts, up_weight, b_up, down_weight, cotangent
):
    sequences, local_len, width = hidden.shape
    half = local_len // 2
    rows = sequences * local_len
    own_rows = rows // 2
    n_f = lax.axis_size("fsdp")
    part = width // n_f
    cols = w_qkv.shape[2]
    f_at = lax.axis_index("fsdp")
    core = lax.axis_index("tp") % 2

    wq, wk, wv = (few(gather_parts(w_qkv[:, i, :]), 0) for i in range(3))
    bias_len = b_qkv.shape[2]
    unit_len = b_up.shape[1]
    vectors = jnp.concatenate(
        [norm_gain.reshape(-1), shifts.reshape(-1), b_qkv.reshape(-1), b_up.reshape(-1)]
    ).reshape(1, -1)
    vectors = jnp.concatenate(gather_parts(vectors), axis=0)
    cuts = [2 * part, 6 * part, 6 * part + 2 * bias_len]
    gains = vectors[:, : cuts[0]].reshape(n_f, 2, part).transpose(1, 0, 2).reshape(2, width)
    shift_rows = vectors[:, cuts[0] : cuts[1]].reshape(n_f, 4, part).transpose(1, 0, 2)
    shift_rows = shift_rows.reshape(4, width).astype(F32)
    gains = gains.astype(F32)
    back = (n_f - f_at) % n_f
    b_pair = vectors[:, cuts[1] : cuts[2]].reshape(n_f, 2, bias_len).transpose(1, 0, 2)
    b_pair = turn(b_pair, 1, back).reshape(2, 1, cols).astype(F32)
    up_bias = turn(vectors[:, cuts[2] :], 0, back).reshape(1, n_f * unit_len).astype(F32)
    w_out_parts = few(gather_parts(w_out), 1)
    up_full = jnp.concatenate(gather_parts(up_weight), axis=0)
    down_full = jnp.concatenate(gather_parts(down_weight), axis=1)

    def localise(value):
        value = turn(value, 2, f_at * part)
        value = turn(value, 1, core * half)
        return value

    x_slots = localise(hidden)
    x_rows = x_slots.reshape(rows, width)
    x_own = x_slots[:, :half].reshape(own_rows, width).astype(F32)
    cot_own = localise(cotangent)[:, :half].reshape(own_rows, width).astype(F32)

    zero_bias = jnp.zeros((1, cols), F32)
    q_all, k_all, v_all = (
        heads_swap(project(x_rows, bias, parts, local_len)).reshape(-1, 2 * HD)
        for bias, parts in ((b_pair[0], wq), (zero_bias, wk), (b_pair[1], wv))
    )
    full_len = q_all.shape[0]
    scal = jnp.concatenate([lengths, (core * half).astype(jnp.int32).reshape(1)])
    attn_all, lse = attend(scal, q_all, k_all, v_all)
    attn_heads = heads_swap(attn_all.reshape(-1, local_len, 2 * HD))
    attn_rows, partial_one = outproj(attn_heads, w_out_parts)

    branch = tp_sum_own(partial_one) + shift_rows[0]
    normed_one, inverse_one = layer_stats(x_own + branch)
    middle = normed_one * gains[0] + shift_rows[1]
    middle_low = share_core(middle.astype(BF16))
    pre_act = mm(middle_low, up_full) + up_bias
    act_low = gelu_value(pre_act).astype(BF16)
    mlp = tp_sum_own(mm(act_low, down_full).astype(BF16)) + shift_rows[2]
    normed_two, inverse_two = layer_stats(middle + mlp)
    result_own = (normed_two * gains[1] + shift_rows[3]).astype(BF16)

    grad_resid_two = norm_back(cot_own, normed_two, inverse_two, gains[1])
    two_low = share_core(grad_resid_two.astype(BF16))
    grad_act = mm(two_low, down_full, NT)
    pre_low = (grad_act * gelu_slope(pre_act)).astype(BF16)
    grad_middle = grad_resid_two + tp_sum_own(mm(pre_low, up_full, NT).astype(BF16))
    grad_down = ctx_sum(scatter_sum(grad_blocks(act_low, two_low, n_f, 1)).astype(BF16))
    grad_up = ctx_sum(scatter_sum(grad_blocks(middle_low, pre_low, n_f, 0)).astype(BF16))

    grad_resid_one = norm_back(grad_middle, normed_one, inverse_one, gains[0])
    one_low = share_core(grad_resid_one.astype(BF16))
    grad_heads = heads_swap(grad_attn(one_low, w_out_parts, local_len)).reshape(full_len, 2 * HD)
    grad_out = ctx_sum(scatter_sum(grad_blocks(attn_rows, one_low, n_f, 1)).astype(BF16))
    grads = attend_back(scal, q_all, k_all, v_all, lse, grad_heads)
    packed = jnp.concatenate([g.reshape(-1, local_len, 2 * HD) for g in grads], axis=1)
    qkv_rows, token_partial = grad_token(heads_swap(packed), (wq, wk, wv), local_len)
    grad_tokens = (grad_resid_one + tp_sum_own(token_partial)).astype(BF16)

    x_halves = x_slots.reshape(sequences, 2, half, width).transpose(1, 0, 2, 3).reshape(rows, width)
    grad_qkv = ctx_sum(scatter_sum(grad_blocks(x_halves, qkv_rows, n_f, 0)).astype(BF16))

    norm_sums = jnp.stack(
        [
            jnp.sum(grad_middle * normed_one, axis=0),
            jnp.sum(cot_own * normed_two, axis=0),
            jnp.sum(grad_resid_one, axis=0),
            jnp.sum(grad_middle, axis=0),
            jnp.sum(grad_resid_two, axis=0),
            jnp.sum(cot_own, axis=0),
        ]
    )
    norm_sums = (norm_sums + swap_core(norm_sums)).reshape(6, n_f, part).transpose(1, 0, 2)
    unit_sums = turn(jnp.sum(pre_low.astype(F32), axis=0).reshape(n_f, unit_len), 0, f_at)
    bias_sums = jnp.sum(qkv_rows.astype(F32), axis=0).reshape(3, n_f, bias_len)
    bias_sums = turn(jnp.stack([bias_sums[0], bias_sums[2]]), 1, f_at).transpose(1, 0, 2)
    small = jnp.concatenate(
        [norm_sums.reshape(n_f, -1), bias_sums.reshape(n_f, -1), unit_sums], axis=1
    )
    small = ctx_sum(scatter_sum([small[d : d + 1] for d in range(n_f)]))
    sums = small[:, : 6 * part].reshape(6, part)
    grad_bias = small[:, 6 * part : 6 * part + 2 * bias_len].reshape(b_qkv.shape)
    grad_unit = small[:, 6 * part + 2 * bias_len :].reshape(b_up.shape)

    def restore(own):
        both = share_core(own).reshape(2, sequences, half, width)
        both = turn(both, 0, core).transpose(1, 0, 2, 3).reshape(sequences, local_len, width)
        return turn(both, 2, ((n_f - f_at) % n_f) * part)

    return (
        restore(result_own),
        restore(grad_tokens),
        grad_qkv.astype(F32).reshape(w_qkv.shape),
        grad_bias,
        grad_out.astype(F32),
        sums[:2],
        sums[2:],
        grad_up.astype(F32),
        grad_unit,
        grad_down.astype(F32),
    )


def solution(mesh):
    in_specs = (
        P("fsdp", "ctx", None),
        P("fsdp"),
        P("fsdp", None, "tp"),
        P(None, "tp", "fsdp"),
        P("tp", "fsdp"),
        P(None, "fsdp"),
        P(None, "fsdp"),
        P("fsdp", "tp"),
        P("tp", "fsdp"),
        P("tp", "fsdp"),
        P("fsdp", "ctx", None),
    )
    out_specs = (
        P("fsdp", "ctx", None),
        P("fsdp", "ctx", None),
        P("fsdp", None, "tp"),
        P(None, "tp", "fsdp"),
        P("tp", "fsdp"),
        P(None, "fsdp"),
        P(None, "fsdp"),
        P("fsdp", "tp"),
        P("tp", "fsdp"),
        P("tp", "fsdp"),
    )
    return jax.shard_map(
        on_device, mesh=mesh, in_specs=in_specs, out_specs=out_specs, check_vma=False
    )
```

```python
import functools

import jax
import jax.numpy as jnp
from jax import lax
from jax.experimental import pallas as pl
from jax.experimental.pallas import tpu as pltpu
from jax.sharding import PartitionSpec as P

HD = 64
EPSILON = 1e-12
NEGATIVE = -1e30
F32 = jnp.float32
BF16 = jnp.bfloat16
VMEM_LIMIT = 32 * 1024 * 1024

NT = (((1,), (1,)), ((), ()))
TN = (((0,), (0,)), ((), ()))
NN = (((1,), (0,)), ((), ()))


def mm(a, b, dims=NN):
    return lax.dot_general(a, b, dims, preferred_element_type=F32)


def swap_core(value):
    n = lax.axis_size("tp")
    return lax.ppermute(value, "tp", [(i, i ^ 1) for i in range(n)])


def swap_y(value):
    n = lax.axis_size("tp")
    return lax.ppermute(value, "tp", [(i, i ^ 2) for i in range(n)])


def gather_parts(value):
    n = lax.axis_size("fsdp")
    parts = [value]
    for d in range(1, n):
        parts.append(lax.ppermute(value, "fsdp", [((i + d) % n, i) for i in range(n)]))
    return parts


def split_gather(value, axis):
    if lax.axis_size("fsdp") != 2:
        return few(gather_parts(value), axis)
    rows = value.shape[0] // 2
    return [value] + [gather_parts(value[i * rows : (i + 1) * rows])[1] for i in range(2)]


def few(parts, axis):
    return parts if len(parts) == 2 else [jnp.concatenate(parts, axis=axis)]


def scatter_start(blocks):
    n = lax.axis_size("fsdp")
    return [blocks[0]] + [
        lax.ppermute(blocks[d], "fsdp", [(i, (i + d) % n) for i in range(n)]) for d in range(1, n)
    ]


def add_kernel(*refs):
    total = refs[0][...].astype(F32)
    for ref in refs[1:-1]:
        total = total + ref[...].astype(F32)
    refs[-1][...] = total.astype(BF16)


def add(*values):
    shape = jax.ShapeDtypeStruct(values[0].shape, BF16)
    return call(add_kernel, shape, n_in=len(values))(*values)


def tie(*values):
    return lax.optimization_barrier(values)


def is_middle():
    place = lax.axis_index("ctx")
    return (place == 1) | (place == 2)


def line_first(value):
    if lax.axis_size("ctx") != 4:
        return value
    return lax.ppermute(value, "ctx", [(0, 1), (3, 2)])


def line_second(value):
    if lax.axis_size("ctx") != 4:
        return lax.psum(value, "ctx")
    return lax.ppermute(value, "ctx", [(1, 2), (2, 1)])


def line_third(value):
    if lax.axis_size("ctx") != 4:
        return value
    return lax.ppermute(value, "ctx", [(1, 0), (2, 3)])


def line_add(value, arrived):
    if lax.axis_size("ctx") != 4:
        return arrived
    return add(value, arrived)


def rest_kernel(n, *refs):
    up_refs, out_refs, small_refs = refs[:n], refs[n : 2 * n], refs[2 * n : 3 * n]
    all_ref = refs[3 * n]
    rows, width = up_refs[0].shape
    half, lanes = out_refs[0].shape[0] // 2, out_refs[0].shape[1]
    all_ref[:rows, :] = sum_of([ref[...].astype(F32) for ref in up_refs]).astype(BF16)
    out = sum_of([ref[...].astype(F32) for ref in out_refs]).astype(BF16)
    all_ref[rows : rows + half, :lanes] = out[:half]
    all_ref[rows : rows + half, lanes : 2 * lanes] = out[half:]
    small = sum_of([ref[...] for ref in small_refs])
    small = jnp.concatenate([small, jnp.zeros_like(small)], axis=0).astype(BF16)
    all_ref[rows + half :, : small.shape[1]] = small
    all_ref[rows + half :, small.shape[1] :] = jnp.zeros((16, width - small.shape[1]), BF16)


def rest_sum(ups, outs, smalls):
    n = len(ups)
    rows, width = ups[0].shape
    shape = (rows + outs[0].shape[0] // 2 + 16, width)
    return call(
        functools.partial(rest_kernel, n), jax.ShapeDtypeStruct(shape, BF16), n_in=3 * n
    )(*ups, *outs, *smalls)


def rest_pick_kernel(scal_ref, sum_ref, third_ref, up_ref, out_ref, small_ref):
    middle = (scal_ref[3] == 1) | (scal_ref[3] == 2)
    rows = up_ref.shape[0]
    half, lanes = out_ref.shape[0] // 2, out_ref.shape[1]

    def fill(ref):
        up_ref[...] = ref[:rows, :].astype(F32)
        out_ref[:half, :] = ref[rows : rows + half, :lanes].astype(F32)
        out_ref[half:, :] = ref[rows : rows + half, lanes : 2 * lanes].astype(F32)
        small_ref[...] = ref[rows + half :, : small_ref.shape[1]].astype(F32)

    pl.when(middle)(lambda: fill(sum_ref))
    pl.when(jnp.logical_not(middle))(lambda: fill(third_ref))


def rest_pick(scal, total, arrived, rows, out_shape):
    width = total.shape[1]
    if lax.axis_size("ctx") != 4:
        arrived = total
    return call(
        rest_pick_kernel,
        (
            jax.ShapeDtypeStruct((rows, width), F32),
            jax.ShapeDtypeStruct(out_shape, F32),
            jax.ShapeDtypeStruct((16, rows), F32),
        ),
        smem=1,
        n_in=3,
    )(scal, total, arrived)


def line_pick(value, arrived):
    if lax.axis_size("ctx") != 4:
        return value
    return jnp.where(is_middle(), value, arrived)


def rotate_out(blocks):
    n = lax.axis_size("ctx")
    return [blocks[0]] + [
        lax.ppermute(blocks[d], "ctx", [(i, (i + d) % n) for i in range(n)]) for d in range(1, n)
    ]


def grad_blocks_kernel(n, axis, n_left, n_right, *refs):
    lefts, rights = refs[:n_left], refs[n_left : n_left + n_right]
    outs = refs[n_left + n_right :]
    rows = min(ref.shape[0] for ref in refs[: n_left + n_right])

    def piece(group, h, cut):
        if len(group) == 1:
            return group[0][h * rows : (h + 1) * rows, cut]
        return group[h][:, cut]

    size = (lefts, rights)[axis][0].shape[1] // n
    for d in range(n):
        cuts = [slice(None), slice(None)]
        cuts[axis] = slice(d * size, (d + 1) * size)
        outs[d][...] = sum_of(
            [mm(piece(lefts, h, cuts[0]), piece(rights, h, cuts[1]), TN) for h in range(2)]
        ).astype(BF16)


def grad_blocks(lefts, rights, n, axis):
    shape = [lefts[0].shape[1], rights[0].shape[1]]
    shape[axis] //= n
    return call(
        functools.partial(grad_blocks_kernel, n, axis, len(lefts), len(rights)),
        [jax.ShapeDtypeStruct(tuple(shape), BF16)] * n,
        n_in=len(lefts) + len(rights),
    )(*lefts, *rights)


def rotate_all(block):
    return rotate_out([block] * lax.axis_size("ctx"))


def rotate_back(blocks):
    n = lax.axis_size("ctx")
    return [blocks[0]] + [
        lax.ppermute(blocks[d], "ctx", [(i, (i - d) % n) for i in range(n)]) for d in range(1, n)
    ]


def tp_pair(own, other):
    pair = add(own, swap_core(other))
    return pair, swap_y(pair)


def share_core(own):
    return jnp.concatenate([own, swap_core(own)], axis=0)


def turn(value, axis, shift):
    size = value.shape[axis]
    doubled = jnp.concatenate([value, value], axis=axis)
    return lax.dynamic_slice_in_dim(doubled, shift, size, axis=axis)


def call(kernel, out_shape, scratch=(), smem=0, n_in=1):
    specs = [pl.BlockSpec(memory_space=pltpu.SMEM)] * smem + [
        pl.BlockSpec(memory_space=pltpu.VMEM)
    ] * (n_in - smem)
    outs = jax.tree.map(lambda _: pl.BlockSpec(memory_space=pltpu.VMEM), out_shape)
    return pl.pallas_call(
        kernel,
        out_shape=out_shape,
        in_specs=specs,
        out_specs=outs,
        scratch_shapes=list(scratch),
        compiler_params=pltpu.CompilerParams(vmem_limit_bytes=VMEM_LIMIT),
        cost_estimate=pl.CostEstimate(flops=1000, bytes_accessed=1000, transcendentals=0),
    )


def lane_low(rows):
    return lax.broadcasted_iota(jnp.int32, (rows, 2 * HD), 1) < HD


def pack_heads(rows_value, heads_ref, base, length):
    low = lane_low(length)
    for tile in range(rows_value.shape[1] // (2 * HD)):
        a = rows_value[:length, tile * 128 : tile * 128 + 128]
        b = rows_value[length:, tile * 128 : tile * 128 + 128]
        even = jnp.where(low, a, pltpu.roll(b, HD, 1))
        odd = jnp.where(low, pltpu.roll(a, HD, 1), b)
        heads_ref[2 * tile, base : base + length, :] = even.astype(BF16)
        heads_ref[2 * tile + 1, base : base + length, :] = odd.astype(BF16)


def unpack_heads(heads_ref, base, length, tile):
    low = lane_low(length)
    even = heads_ref[2 * tile, base : base + length, :].astype(F32)
    odd = heads_ref[2 * tile + 1, base : base + length, :].astype(F32)
    a = jnp.where(low, even, pltpu.roll(odd, HD, 1))
    b = jnp.where(low, pltpu.roll(even, HD, 1), odd)
    return a, b


def turned(scal_ref, d, n):
    return lax.rem(scal_ref[3] + d, n)


def project_kernel(n_parts, n, length, *refs):
    scal_ref, x_ref, bias_ref = refs[:3]
    w_refs = refs[3 : 3 + n_parts]
    out_refs = refs[3 + n_parts : 3 + n_parts + n]
    heads_ref = refs[-1]
    block = w_refs[0].shape[0]
    cols = n * HD
    for kind in range(3):
        cut = slice(kind * cols, (kind + 1) * cols)
        acc = mm(x_ref[:, :block], w_refs[0][:, cut])
        for d in range(1, n_parts):
            acc += mm(x_ref[:, d * block : (d + 1) * block], w_refs[d][:, cut])
        if kind != 1:
            acc += bias_ref[kind // 2 : kind // 2 + 1, :]
        pack_heads(acc, heads_ref, kind * length, length)
    for d in range(n):
        out_refs[d][...] = heads_ref[turned(scal_ref, d, n)]


def project(scal, x, bias, parts, length):
    n = parts[0].shape[1] // (3 * HD)
    kernel = functools.partial(project_kernel, len(parts), n, length)
    shape = jax.ShapeDtypeStruct((3 * length, 2 * HD), BF16)
    return call(
        kernel,
        [shape] * n,
        scratch=[pltpu.VMEM((n, 3 * length, 2 * HD), BF16)],
        smem=1,
        n_in=3 + len(parts),
    )(scal, x, bias, *parts)


def assemble(refs, start, length):
    return jnp.concatenate([ref[start : start + length, :] for ref in refs], axis=0)


def masked_sides(scal_ref, slot, q, k, n):
    rows = q.shape[0]
    length = rows // n
    lane = lax.broadcasted_iota(jnp.int32, (rows, 2 * HD), 1)
    spare = HD * (1 - slot)
    mine = (lane >= slot * HD) & (lane < slot * HD + HD)
    q_side = jnp.where(mine, q.astype(F32) * (HD ** -0.5), 0.0)
    q_side = jnp.where(lane == spare, 1.0, q_side).astype(BF16)
    place = lax.broadcasted_iota(jnp.int32, (length, 2 * HD), 0) + scal_ref[2]
    place = jnp.where(place >= length, place - length, place)
    place = jnp.concatenate([place + length * turned(scal_ref, n - d, n) for d in range(n)], axis=0)
    bias = jnp.where(place < scal_ref[slot], 0.0, NEGATIVE)
    k_side = jnp.where(lane == spare, bias, k.astype(F32)).astype(BF16)
    return q_side, k_side


def attend_kernel(block, n, *refs):
    scal_ref = refs[0]
    q_val, k_val, v_val = (assemble(refs[1 : 1 + n], i * block, block) for i in range(3))
    out_refs = refs[1 + n : 1 + 2 * n]
    lse_ref, all_ref = refs[1 + 2 * n :]
    length = q_val.shape[0]
    for i, value in enumerate((q_val, k_val, v_val)):
        all_ref[i] = value
    v_t = v_val.astype(F32).T.astype(BF16)
    sides = [masked_sides(scal_ref, s, q_val, k_val, n) for s in range(2)]
    low = lax.broadcasted_iota(jnp.int32, (2 * HD, block), 0) < HD
    for i, start in enumerate(range(0, length, block)):
        results = []
        for s in range(2):
            q_side, k_side = sides[s]
            scores = mm(k_side, q_side[start : start + block], NT)
            peak = jnp.max(scores, axis=0, keepdims=True)
            weights = jnp.exp(scores - peak)
            total = jnp.sum(weights, axis=0, keepdims=True)
            res = mm(v_t, weights.astype(BF16))
            results.append(res * (1.0 / total))
            lse_ref[s : s + 1, start : start + block] = peak + jnp.log(total)
        both = jnp.where(low, results[0], results[1])
        out_refs[i][...] = both.T.astype(BF16)


def attend(scal, parts):
    n = len(parts)
    block = parts[0].shape[0] // 3
    return call(
        functools.partial(attend_kernel, block, n),
        [jax.ShapeDtypeStruct((block, 2 * HD), BF16)] * n
        + [
            jax.ShapeDtypeStruct((2, n * block), F32),
            jax.ShapeDtypeStruct((3, n * block, 2 * HD), BF16),
        ],
        smem=1,
        n_in=1 + n,
    )(scal, *parts)


def attend_back_kernel(block, n, *refs):
    scal_ref = refs[0]
    all_ref, lse_ref = refs[1:3]
    q_val, k_val, v_val = all_ref[0], all_ref[1], all_ref[2]
    g_val = assemble(refs[3 : 3 + n], 0, block)
    out_refs = refs[3 + n : 3 + 2 * n]
    p_ref, s_ref = refs[3 + 2 * n :]
    length = q_val.shape[0]
    scale = HD ** -0.5
    k_t = k_val.astype(F32).T.astype(BF16)
    lane = lax.broadcasted_iota(jnp.int32, (length, 2 * HD), 1)
    low_t = lax.broadcasted_iota(jnp.int32, (2 * HD, block), 0) < HD
    low = lane < HD
    keep_q = []
    keep_k = []
    keep_v = []
    for s in range(2):
        q_side, k_side = masked_sides(scal_ref, s, q_val, k_val, n)
        mine = low if s == 0 else ~low
        g_side = jnp.where(mine, g_val.astype(F32), 0.0).astype(BF16)
        grads_q = []
        for start in range(0, length, block):
            scores = mm(k_side, q_side[start : start + block], NT)
            probs = jnp.exp(scores - lse_ref[s : s + 1, start : start + block])
            grad_probs = mm(v_val, g_side[start : start + block], NT)
            delta = jnp.sum(grad_probs * probs, axis=0, keepdims=True)
            grad_scores = (probs * (grad_probs - delta)).astype(BF16)
            p_ref[:, start : start + block] = probs.astype(BF16)
            s_ref[:, start : start + block] = grad_scores
            grads_q.append(mm(k_t, grad_scores))
        keep_q.append(grads_q)
        keep_v.append(mm(p_ref[...], g_val))
        keep_k.append(mm(s_ref[...], q_val))
    grad_k = jnp.where(low, keep_k[0], keep_k[1]) * scale
    grad_v = jnp.where(low, keep_v[0], keep_v[1])
    for i in range(n):
        cut = slice(i * block, (i + 1) * block)
        both = jnp.where(low_t, keep_q[0][i], keep_q[1][i]) * scale
        out_refs[i][:block, :] = both.T.astype(BF16)
        out_refs[i][block : 2 * block, :] = grad_k[cut].astype(BF16)
        out_refs[i][2 * block :, :] = grad_v[cut].astype(BF16)


def attend_back(scal, qkv, lse, grad):
    n = len(grad)
    block = grad[0].shape[0]
    length = n * block
    return call(
        functools.partial(attend_back_kernel, block, n),
        [jax.ShapeDtypeStruct((3 * block, 2 * HD), BF16)] * n,
        scratch=[pltpu.VMEM((length, length), BF16), pltpu.VMEM((length, length), BF16)],
        smem=1,
        n_in=3 + n,
    )(scal, qkv, lse, *grad)


def outproj_kernel(n_parts, n, length, *refs):
    scal_ref = refs[0]
    in_refs = refs[1 : 1 + n]
    w_refs = refs[1 + n : 1 + n + n_parts]
    attn_ref, own_ref, other_ref, heads_ref = refs[1 + n + n_parts :]
    half = length // 2
    for d in range(n):
        heads_ref[turned(scal_ref, d, n)] = in_refs[d][...]
    for tile in range(n // 2):
        for s, value in enumerate(unpack_heads(heads_ref, 0, length, tile)):
            for h in range(2):
                at = h * length + s * half
                attn_ref[at : at + half, tile * 128 : tile * 128 + 128] = value[
                    h * half : (h + 1) * half
                ].astype(BF16)
    block = w_refs[0].shape[1]
    for d in range(n_parts):
        part = mm(attn_ref[...], w_refs[d][...]).astype(BF16)
        own_ref[:, d * block : (d + 1) * block] = part[:length]
        other_ref[:, d * block : (d + 1) * block] = part[length:]


def outproj(scal, heads, parts):
    n = len(heads)
    length = heads[0].shape[0]
    rows, cols = 2 * length, n * HD
    width = parts[0].shape[1] * len(parts)
    return call(
        functools.partial(outproj_kernel, len(parts), n, length),
        (
            jax.ShapeDtypeStruct((rows, cols), BF16),
            jax.ShapeDtypeStruct((length, width), BF16),
            jax.ShapeDtypeStruct((length, width), BF16),
        ),
        scratch=[pltpu.VMEM((n, length, 2 * HD), BF16)],
        smem=1,
        n_in=1 + n + len(parts),
    )(scal, *heads, *parts)


def grad_attn_kernel(n_parts, n, length, *refs):
    scal_ref, own_ref, other_ref = refs[:3]
    w_refs = refs[3 : 3 + n_parts]
    out_refs = refs[3 + n_parts : 3 + n_parts + n]
    heads_ref = refs[-1]
    half = length // 2
    block = w_refs[0].shape[1]
    for h, g_ref in enumerate((own_ref, other_ref)):
        acc = mm(g_ref[:, :block], w_refs[0][...], NT)
        for d in range(1, n_parts):
            acc += mm(g_ref[:, d * block : (d + 1) * block], w_refs[d][...], NT)
        pack_heads(acc, heads_ref, h * half, half)
    for d in range(n):
        out_refs[d][...] = heads_ref[turned(scal_ref, d, n)]


def grad_attn(scal, own, other, parts, length):
    n = parts[0].shape[0] // HD
    return call(
        functools.partial(grad_attn_kernel, len(parts), n, length),
        [jax.ShapeDtypeStruct((length, 2 * HD), BF16)] * n,
        scratch=[pltpu.VMEM((n, length, 2 * HD), BF16)],
        smem=1,
        n_in=3 + len(parts),
    )(scal, own, other, *parts)


def grad_token_kernel(n_parts, n, length, *refs):
    scal_ref = refs[0]
    in_refs = refs[1 : 1 + n]
    w_refs = refs[1 + n : 1 + n + n_parts]
    own_ref, other_ref, rows_ref, heads_ref = refs[1 + n + n_parts :]
    half = length // 2
    cols = n * HD
    for d in range(n):
        heads_ref[turned(scal_ref, d, n)] = in_refs[d][...]
    for kind in range(3):
        for tile in range(n // 2):
            lane = kind * cols + tile * 128
            for s, value in enumerate(unpack_heads(heads_ref, kind * length, length, tile)):
                rows_ref[s * length : (s + 1) * length, lane : lane + 128] = value.astype(BF16)
    block = w_refs[0].shape[0]
    for d in range(n_parts):
        acc = mm(rows_ref[...], w_refs[d][...], NT)
        for s in range(2):
            for h in range(2):
                at = s * length + h * half
                (own_ref, other_ref)[h][
                    s * half : (s + 1) * half, d * block : (d + 1) * block
                ] = acc[at : at + half].astype(BF16)


def grad_token(scal, heads, parts):
    n = len(heads)
    length = heads[0].shape[0] // 3
    n_parts = len(parts)
    width = parts[0].shape[0] * n_parts
    return call(
        functools.partial(grad_token_kernel, n_parts, n, length),
        (
            jax.ShapeDtypeStruct((length, width), BF16),
            jax.ShapeDtypeStruct((length, width), BF16),
        ),
        scratch=[
            pltpu.VMEM((2 * length, 3 * n * HD), BF16),
            pltpu.VMEM((n, 3 * length, 2 * HD), BF16),
        ],
        smem=1,
        n_in=1 + n + n_parts,
    )(scal, *heads, *parts)


def grad_project_kernel(n_f, n, length, *refs):
    scal_ref, own_ref, other_ref = refs[:3]
    in_refs = refs[3 : 3 + n]
    out_refs = refs[3 + n : 3 + n + n_f]
    half = length // 2
    low = lane_low(half)
    total = None
    sums = None
    for d in range(n):
        at = turned(scal_ref, n - d, n)
        for h, x_ref in enumerate((own_ref, other_ref)):
            dq, dk, dv = (
                in_refs[d][kind * length + h * half : kind * length + (h + 1) * half, :].astype(F32)
                for kind in range(3)
            )
            first = [
                jnp.where(low, dq, pltpu.roll(dk, HD, 1)),
                jnp.where(low, pltpu.roll(dq, HD, 1), dk),
            ]
            second = [jnp.where(low, dv, 0.0), jnp.where(low, pltpu.roll(dv, HD, 1), 0.0)]
            rows = jnp.concatenate(
                [jnp.concatenate(first, axis=0), jnp.concatenate(second, axis=0)], axis=1
            )
            add = column_sum(rows)
            term = mm(rows.T.astype(BF16), x_ref[at])
            total = term if total is None else total + term
            sums = add if sums is None else sums + add
    width = total.shape[1]
    part = width // n_f
    for d in range(n_f):
        out = out_refs[d]
        out[:part, :] = total[:, d * part : (d + 1) * part].T.astype(out.dtype)
        out[part:, :] = jnp.broadcast_to(sums, (16, sums.shape[1])).astype(out.dtype)


def grad_project(scal, x_own, x_other, heads, n_f):
    n = len(heads)
    length = heads[0].shape[0] // 3
    shape = (x_own.shape[2] // n_f + 16, 4 * HD)
    return call(
        functools.partial(grad_project_kernel, n_f, n, length),
        [jax.ShapeDtypeStruct(shape, BF16)] * n_f,
        smem=1,
        n_in=3 + n,
    )(scal, x_own, x_other, *heads)


def spread_heads_kernel(n, *refs):
    scal_ref = refs[0]
    in_refs = refs[1 : 1 + n]
    q_ref, k_ref, v_ref, bias_ref, heads_ref = refs[1 + n :]
    rows = heads_ref.shape[1]
    part = q_ref.shape[0]
    low = lane_low(rows)
    for d in range(n):
        heads_ref[turned(scal_ref, n - d, n)] = in_refs[d][...].astype(F32)
    for tile in range(n // 2):
        cut = slice(tile * 128, tile * 128 + 128)
        a, b = heads_ref[2 * tile, :, :128], heads_ref[2 * tile + 1, :, :128]
        q_val = jnp.where(low, a, pltpu.roll(b, HD, 1))
        k_val = jnp.where(low, pltpu.roll(a, HD, 1), b)
        a, b = heads_ref[2 * tile, :, 128:], heads_ref[2 * tile + 1, :, 128:]
        v_val = jnp.where(low, a, pltpu.roll(b, HD, 1))
        q_ref[:, cut] = q_val[:part]
        k_ref[:, cut] = k_val[:part]
        v_ref[:, cut] = v_val[:part]
        bias_ref[0:1, cut] = q_val[part : part + 1]
        bias_ref[1:2, cut] = v_val[part : part + 1]


def spread_heads(scal, parts):
    n = len(parts)
    rows = parts[0].shape[0]
    shape = jax.ShapeDtypeStruct((rows - 16, n * HD), F32)
    return call(
        functools.partial(spread_heads_kernel, n),
        (shape, shape, shape, jax.ShapeDtypeStruct((2, n * HD), F32)),
        scratch=[pltpu.VMEM((n, rows, 4 * HD), F32)],
        smem=1,
        n_in=1 + n,
    )(scal, *parts)


def pieces(size, count):
    step = size // count
    return [slice(i * step, (i + 1) * step) for i in range(count)]


def mean_of(values):
    return jnp.mean(values, axis=-1, keepdims=True)


def layer_stats(values):
    shifted = values - mean_of(values)
    inverse = lax.rsqrt(mean_of(shifted * shifted) + EPSILON)
    return (shifted * inverse, inverse)


def norm_back(grad_norm, normed, inverse, gain_row):
    scaled = grad_norm * gain_row
    return inverse * (scaled - mean_of(scaled) - normed * mean_of(scaled * normed))


def column_sum(values):
    return jnp.sum(values, axis=0, keepdims=True)


def first_norm_kernel(
    x_ref, pair_ref, far_ref, gain_ref, shift_ref, mid_ref, normed_ref, inverse_ref, low_ref
):
    branch = pair_ref[...].astype(F32) + far_ref[...].astype(F32) + shift_ref[0:1, :]
    normed, inverse = layer_stats(x_ref[...].astype(F32) + branch)
    middle = normed * gain_ref[0:1, :] + shift_ref[1:2, :]
    mid_ref[...] = middle
    normed_ref[...] = normed
    inverse_ref[...] = jnp.broadcast_to(inverse, inverse_ref.shape)
    low_ref[...] = middle.astype(BF16)


def first_norm(x, pair, far, gains, shift_rows):
    full = jax.ShapeDtypeStruct(x.shape, F32)
    return call(
        first_norm_kernel,
        (
            full,
            full,
            jax.ShapeDtypeStruct((x.shape[0], 128), F32),
            jax.ShapeDtypeStruct(x.shape, BF16),
        ),
        n_in=5,
    )(x, pair, far, gains, shift_rows)


def second_norm_kernel(
    mid_ref, pair_ref, far_ref, gain_ref, shift_ref, cot_ref, out_ref, grad_ref, low_ref, sum_ref
):
    mlp = pair_ref[...].astype(F32) + far_ref[...].astype(F32) + shift_ref[2:3, :]
    normed, inverse = layer_stats(mid_ref[...] + mlp)
    out_ref[...] = (normed * gain_ref[1:2, :] + shift_ref[3:4, :]).astype(BF16)
    cot = cot_ref[...].astype(F32)
    grad = norm_back(cot, normed, inverse, gain_ref[1:2, :])
    grad_ref[...] = grad
    low_ref[...] = grad.astype(BF16)
    sum_ref[0:1, :] = column_sum(cot * normed)
    sum_ref[1:2, :] = column_sum(grad)
    sum_ref[2:3, :] = column_sum(cot)


def second_norm(mid, pair, far, gains, shift_rows, cot):
    low = jax.ShapeDtypeStruct(mid.shape, BF16)
    return call(
        second_norm_kernel,
        (
            low,
            jax.ShapeDtypeStruct(mid.shape, F32),
            low,
            jax.ShapeDtypeStruct((3, mid.shape[1]), F32),
        ),
        n_in=6,
    )(mid, pair, far, gains, shift_rows, cot)


def first_back_kernel(
    two_ref, pair_ref, far_ref, normed_ref, inverse_ref, gain_ref, grad_ref, low_ref, sum_ref
):
    grad_mid = two_ref[...] + (pair_ref[...].astype(F32) + far_ref[...].astype(F32))
    normed = normed_ref[...]
    grad = norm_back(grad_mid, normed, inverse_ref[:, 0:1], gain_ref[0:1, :])
    grad_ref[...] = grad
    low_ref[...] = grad.astype(BF16)
    sum_ref[0:1, :] = column_sum(grad_mid * normed)
    sum_ref[1:2, :] = column_sum(grad)
    sum_ref[2:3, :] = column_sum(grad_mid)


def first_back(two, pair, far, normed, inverse, gains):
    return call(
        first_back_kernel,
        (
            jax.ShapeDtypeStruct(two.shape, F32),
            jax.ShapeDtypeStruct(two.shape, BF16),
            jax.ShapeDtypeStruct((3, two.shape[1]), F32),
        ),
        n_in=6,
    )(two, pair, far, normed, inverse, gains)


def last_sum_kernel(one_ref, pair_ref, far_ref, out_ref):
    total = pair_ref[...].astype(F32) + far_ref[...].astype(F32)
    out_ref[...] = (one_ref[...] + total).astype(BF16)


def row_cuts(refs):
    cuts = []
    start = 0
    for ref in refs:
        cuts.append((slice(start, start + ref.shape[0]), ref))
        start += ref.shape[0]
    return cuts


def column_groups(refs):
    groups = []
    column = 0
    for group in (refs[:1], refs[1:]):
        if group:
            width = group[0].shape[1]
            groups.append((slice(column, column + width), row_cuts(group)))
            column += width
    return groups


def sum_of(terms):
    total = terms[0]
    for term in terms[1:]:
        total = total + term
    return total


def feed_kernel(n_parts, *refs):
    own_ref, other_ref, bias_ref = refs[:3]
    ups = row_cuts(refs[3 : 3 + n_parts])
    downs = column_groups(refs[3 + n_parts : 3 + 2 * n_parts])
    pre_ref, act_ref, part_refs = refs[3 + 2 * n_parts], refs[4 + 2 * n_parts], refs[-2:]
    rows = own_ref.shape[0]
    for h, in_ref in enumerate((own_ref, other_ref)):
        pre = sum_of([mm(in_ref[:, cut], ref[...]) for cut, ref in ups]) + bias_ref[...]
        act = gelu_value(pre).astype(BF16)
        pre_ref[h * rows : (h + 1) * rows, :] = pre
        act_ref[h * rows : (h + 1) * rows, :] = act
        for columns, pieces in downs:
            part = sum_of([mm(act[:, cut], ref[...]) for cut, ref in pieces])
            part_refs[h][:, columns] = part.astype(BF16)


def feed(own, other, bias, ups, downs):
    rows, width = own.shape
    units = bias.shape[1]
    part = jax.ShapeDtypeStruct((rows, width), BF16)
    return call(
        functools.partial(feed_kernel, len(ups)),
        (
            jax.ShapeDtypeStruct((2 * rows, units), F32),
            jax.ShapeDtypeStruct((2 * rows, units), BF16),
            part,
            part,
        ),
        n_in=3 + 2 * len(ups),
    )(own, other, bias, *ups, *downs)


def feed_back_kernel(n_parts, *refs):
    own_ref, other_ref, pre_ref = refs[:3]
    ups = row_cuts(refs[3 : 3 + n_parts])
    downs = column_groups(refs[3 + n_parts : 3 + 2 * n_parts])
    low_ref, sum_ref, part_refs = refs[3 + 2 * n_parts], refs[4 + 2 * n_parts], refs[-2:]
    rows = own_ref.shape[0]
    sums = []
    for h, in_ref in enumerate((own_ref, other_ref)):
        terms = []
        for columns, pieces in downs:
            grads = [mm(in_ref[:, columns], ref[...], NT) for _, ref in pieces]
            terms.append(grads[0] if len(grads) == 1 else jnp.concatenate(grads, axis=1))
        grad = sum_of(terms)
        low = (grad * gelu_slope(pre_ref[h * rows : (h + 1) * rows, :])).astype(BF16)
        low_ref[h * rows : (h + 1) * rows, :] = low
        sums.append(column_sum(low.astype(F32)))
        for cut, ref in ups:
            part_refs[h][:, cut] = mm(low, ref[...], NT).astype(BF16)
    sum_ref[...] = sums[0] + sums[1]


def feed_back(own, other, pre, ups, downs):
    rows, width = own.shape
    units = pre.shape[1]
    part = jax.ShapeDtypeStruct((rows, width), BF16)
    return call(
        functools.partial(feed_back_kernel, len(ups)),
        (
            jax.ShapeDtypeStruct((2 * rows, units), BF16),
            jax.ShapeDtypeStruct((1, units), F32),
            part,
            part,
        ),
        n_in=3 + 2 * len(ups),
    )(own, other, pre, *ups, *downs)


def gelu_value(values):
    return 0.5 * values * (1.0 + lax.erf(values * 0.7071067811865476))


def gelu_slope(values):
    return (
        0.5 * (1.0 + lax.erf(values * 0.7071067811865476))
        + values * jnp.exp(-0.5 * values * values) * 0.3989422804014327
    )


def on_device(
    hidden, lengths, w_qkv, b_qkv, w_out, norm_gain, shifts, up_weight, b_up, down_weight, cotangent
):
    sequences, local_len, width = hidden.shape
    half = local_len // 2
    rows = sequences * local_len
    own_rows = rows // 2
    n_f = lax.axis_size("fsdp")
    part = width // n_f
    cols = w_qkv.shape[2]
    f_at = lax.axis_index("fsdp")
    core = lax.axis_index("tp") % 2

    w_parts = few(gather_parts(w_qkv.reshape(part, 3 * cols)), 0)
    bias_len = b_qkv.shape[2]
    unit_len = b_up.shape[1]
    vectors = jnp.concatenate(
        [norm_gain.reshape(-1), shifts.reshape(-1), b_qkv.reshape(-1), b_up.reshape(-1)]
    ).reshape(1, -1)
    vectors = jnp.concatenate(gather_parts(vectors), axis=0)
    cuts = [2 * part, 6 * part, 6 * part + 2 * bias_len]
    gains = vectors[:, : cuts[0]].reshape(n_f, 2, part).transpose(1, 0, 2).reshape(2, width)
    shift_rows = vectors[:, cuts[0] : cuts[1]].reshape(n_f, 4, part).transpose(1, 0, 2)
    shift_rows = shift_rows.reshape(4, width).astype(F32)
    gains = gains.astype(F32)
    back = (n_f - f_at) % n_f
    b_pair = vectors[:, cuts[1] : cuts[2]].reshape(n_f, 2, bias_len).transpose(1, 0, 2)
    b_pair = turn(b_pair, 1, back).reshape(2, cols).astype(F32)
    up_bias = turn(vectors[:, cuts[2] :], 0, back).reshape(1, n_f * unit_len).astype(F32)
    w_out, up_weight, down_weight, _ = tie(w_out, up_weight, down_weight, w_parts[-1])
    w_out_parts = few(gather_parts(w_out), 1)
    up_pieces = split_gather(up_weight, 0)
    down_pieces = split_gather(down_weight, 1)

    def localise(value):
        value = turn(value, 2, f_at * part)
        value = turn(value, 1, core * half)
        return value

    x_slots = localise(hidden)
    x_rows = x_slots.reshape(rows, width)
    x_own = x_slots[:, :half].reshape(own_rows, width)
    cot_own = localise(cotangent)[:, :half].reshape(own_rows, width)

    scal = jnp.concatenate(
        [
            lengths,
            (core * half).astype(jnp.int32).reshape(1),
            lax.axis_index("ctx").astype(jnp.int32).reshape(1),
        ]
    )
    heads = rotate_out(project(scal, x_rows, b_pair, w_parts, local_len))
    heads, up_pieces[1:2] = tie(heads, up_pieces[1:2])
    *attn_parts, lse, qkv_all = attend(scal, heads)
    x_own, _ = tie(x_own, attn_parts[0])
    x_all_own = lax.all_gather(x_own, "ctx", axis=0)
    x_all_other = swap_core(x_all_own)
    heads, up_pieces[2:] = tie(rotate_back(attn_parts), up_pieces[2:])
    attn_rows, own, other = outproj(scal, heads, w_out_parts)

    other, down_pieces[1:2] = tie(swap_core(other), down_pieces[1:2])
    pair = add(own, other)
    far, down_pieces[2:] = tie(swap_y(pair), down_pieces[2:])
    middle, normed_one, inverse_one, mid_own = first_norm(
        x_own, pair, far, gains, shift_rows
    )
    mid_other = swap_core(mid_own)
    pre_act, act_low, *partial = feed(mid_own, mid_other, up_bias, up_pieces, down_pieces)

    result_own, grad_two, two_own, two_sums = second_norm(
        middle, *tp_pair(*partial), gains, shift_rows, cot_own
    )
    two_other = swap_core(two_own)
    down_blocks = grad_blocks([act_low], [two_own, two_other], n_f, 1)
    two_own, down_blocks = tie(two_own, down_blocks)
    down_blocks = scatter_start(down_blocks)
    pre_low, unit_sums, *partial = feed_back(two_own, two_other, pre_act, up_pieces, down_pieces)
    pair, far = tp_pair(*partial)
    up_blocks = list(grad_blocks([mid_own, mid_other], [pre_low], n_f, 0))
    far, up_blocks[0] = tie(far, up_blocks[0])
    up_blocks = scatter_start(up_blocks)

    grad_one, one_own, one_sums = first_back(grad_two, pair, far, normed_one, inverse_one, gains)
    one_other = swap_core(one_own)
    norm_sums = jnp.concatenate([one_sums, two_sums], axis=0)
    norm_sums = norm_sums + swap_core(norm_sums)
    unit_sums = turn(unit_sums, 1, f_at * unit_len)
    small = jnp.concatenate([norm_sums, unit_sums, jnp.zeros_like(unit_sums)], axis=0)
    small = scatter_start([small[:, d * part : (d + 1) * part] for d in range(n_f)])
    out_blocks = scatter_start(grad_blocks([attn_rows], [one_own, one_other], n_f, 1))
    grad_parts = grad_attn(scal, one_own, one_other, w_out_parts, local_len)

    grad_heads, down_blocks = tie(rotate_out(grad_parts), down_blocks)
    down_sum = add(*down_blocks)
    down_step = line_first(down_sum)
    grad_heads, down_sum, x_all_other = tie(grad_heads, down_sum, x_all_other)
    head_grads = attend_back(scal, qkv_all, lse, grad_heads)
    qkv_blocks = scatter_start(grad_project(scal, x_all_own, x_all_other, head_grads, n_f))
    head_rows, down_step, up_blocks, out_blocks, small, qkv_blocks = tie(
        rotate_back(head_grads), down_step, up_blocks, out_blocks, small, qkv_blocks
    )

    rest = rest_sum(up_blocks, out_blocks, small)
    rest_step = line_first(rest)
    down_sum = line_add(down_sum, down_step)
    down_step = line_second(down_sum)
    head_rows, rest_step, down_step, qkv_parts = tie(
        head_rows, rest_step, down_step, rotate_all(add(*qkv_blocks))
    )

    rest = line_add(rest, rest_step)
    rest_step = line_second(rest)
    down_sum = line_add(down_sum, down_step)
    down_step = line_third(down_sum)
    own, other = grad_token(scal, head_rows, w_parts)
    pair, far = tp_pair(own, other)
    far, rest_step, down_step = tie(far, rest_step, down_step)

    rest = line_add(rest, rest_step)
    rest_step = line_third(rest)
    grad_tokens = call(last_sum_kernel, jax.ShapeDtypeStruct(one_own.shape, BF16), n_in=3)(
        grad_one, pair, far
    )
    grad_q, grad_k, grad_v, grad_bias = spread_heads(scal, qkv_parts)
    grad_qkv = jnp.stack([grad_q, grad_k, grad_v], axis=1)
    grad_bias = lax.dynamic_slice_in_dim(grad_bias, f_at * bias_len, bias_len, axis=1)
    grad_bias = grad_bias.reshape(b_qkv.shape)

    grad_down = line_pick(down_sum, down_step)
    grad_up, grad_out, small = rest_pick(scal, rest, rest_step, part, w_out.shape)
    grad_gain = jnp.stack([small[0], small[3]])
    grad_shift = jnp.stack([small[1], small[2], small[4], small[5]])
    grad_unit = small[6].reshape(b_up.shape)

    def restore(own):
        both = share_core(own).reshape(2, sequences, half, width)
        both = turn(both, 0, core).transpose(1, 0, 2, 3).reshape(sequences, local_len, width)
        return turn(both, 2, ((n_f - f_at) % n_f) * part)

    return (
        restore(result_own),
        restore(grad_tokens),
        grad_qkv,
        grad_bias,
        grad_out.astype(F32),
        grad_gain,
        grad_shift,
        grad_up.astype(F32),
        grad_unit,
        grad_down.astype(F32),
    )


def solution(mesh):
    in_specs = (
        P("fsdp", "ctx", None),
        P("fsdp"),
        P("fsdp", None, "tp"),
        P(None, "tp", "fsdp"),
        P("tp", "fsdp"),
        P(None, "fsdp"),
        P(None, "fsdp"),
        P("fsdp", "tp"),
        P("tp", "fsdp"),
        P("tp", "fsdp"),
        P("fsdp", "ctx", None),
    )
    out_specs = (
        P("fsdp", "ctx", None),
        P("fsdp", "ctx", None),
        P("fsdp", None, "tp"),
        P(None, "tp", "fsdp"),
        P("tp", "fsdp"),
        P(None, "fsdp"),
        P(None, "fsdp"),
        P("fsdp", "tp"),
        P("tp", "fsdp"),
        P("tp", "fsdp"),
    )
    return jax.shard_map(
        on_device, mesh=mesh, in_specs=in_specs, out_specs=out_specs, check_vma=False
    )
```

```python
import functools

import jax
import jax.numpy as jnp
from jax import lax
from jax.experimental import pallas as pl
from jax.experimental.pallas import tpu as pltpu
from jax.sharding import PartitionSpec as P

HD = 64
EPSILON = 1e-12
NEGATIVE = -1e30
F32 = jnp.float32
BF16 = jnp.bfloat16
VMEM_LIMIT = 32 * 1024 * 1024

NT = (((1,), (1,)), ((), ()))
TN = (((0,), (0,)), ((), ()))
NN = (((1,), (0,)), ((), ()))


def mm(a, b, dims=NN):
    return lax.dot_general(a, b, dims, preferred_element_type=F32)


def swap_core(value):
    n = lax.axis_size("tp")
    return lax.ppermute(value, "tp", [(i, i ^ 1) for i in range(n)])


def swap_y(value):
    n = lax.axis_size("tp")
    return lax.ppermute(value, "tp", [(i, i ^ 2) for i in range(n)])


def gather_parts(value):
    n = lax.axis_size("fsdp")
    parts = [value]
    for d in range(1, n):
        parts.append(lax.ppermute(value, "fsdp", [((i + d) % n, i) for i in range(n)]))
    return parts


def split_rows(value):
    if lax.axis_size("fsdp") != 2:
        return [value]
    rows = value.shape[0] // 2
    return [value[:rows], value[rows:]]


def split_gather(value, pieces, axis):
    if len(pieces) == 1:
        return few(gather_parts(pieces[0]), axis)
    return [value] + [gather_parts(piece)[1] for piece in pieces]


def few(parts, axis):
    return parts if len(parts) == 2 else [jnp.concatenate(parts, axis=axis)]


def scatter_start(blocks):
    n = lax.axis_size("fsdp")
    return [blocks[0]] + [
        lax.ppermute(blocks[d], "fsdp", [(i, (i + d) % n) for i in range(n)]) for d in range(1, n)
    ]


def add_kernel(*refs):
    total = refs[0][...].astype(F32)
    for ref in refs[1:-1]:
        total = total + ref[...].astype(F32)
    refs[-1][...] = total.astype(BF16)


def add(*values, after=()):
    shape = jax.ShapeDtypeStruct(values[0].shape, BF16)
    return call(add_kernel, shape, n_in=len(values), after=after)(*values)


def tie(*values):
    return lax.optimization_barrier(values)


def is_middle():
    place = lax.axis_index("ctx")
    return (place == 1) | (place == 2)


def line_first(value):
    if lax.axis_size("ctx") != 4:
        return value
    return lax.ppermute(value, "ctx", [(0, 1), (3, 2)])


def line_second(value):
    if lax.axis_size("ctx") != 4:
        return lax.psum(value, "ctx")
    return lax.ppermute(value, "ctx", [(1, 2), (2, 1)])


def line_third(value):
    if lax.axis_size("ctx") != 4:
        return value
    return lax.ppermute(value, "ctx", [(1, 0), (2, 3)])


def line_add(value, arrived, after=()):
    if lax.axis_size("ctx") != 4:
        return arrived
    return add(value, arrived, after=after)


def out_blocks_kernel(n, attn_ref, own_ref, other_ref, sums_ref, far_sums_ref, unit_ref, *outs):
    half = own_ref.shape[0]
    rows = attn_ref.shape[1]
    sums = sums_ref[...] + far_sums_ref[...]
    width = sums.shape[1]
    sums = jnp.concatenate(
        [sums, unit_ref[...], jnp.zeros((15 - sums.shape[0], width), F32)], axis=0
    ).astype(BF16)
    size = width // n
    for d in range(n):
        cut = slice(d * size, (d + 1) * size)
        total = mm(attn_ref[:half, :], own_ref[:, cut], TN)
        total += mm(attn_ref[half:, :], other_ref[:, cut], TN)
        outs[d][:rows, :] = total.astype(BF16)
        outs[d][rows:, :] = sums[:, cut]


def out_gradient(attn, own, other, sums, far_sums, units, n, after):
    shape = (attn.shape[1] + 16, own.shape[1] // n)
    return call(
        functools.partial(out_blocks_kernel, n),
        [jax.ShapeDtypeStruct(shape, BF16)] * n,
        n_in=6,
        after=after,
    )(attn, own, other, sums, far_sums, units)


def rest_kernel(n, *refs):
    up_refs, out_refs = refs[:n], refs[n : 2 * n]
    all_ref = refs[2 * n]
    rows, width = up_refs[0].shape
    half, lanes = (out_refs[0].shape[0] - 16) // 2, out_refs[0].shape[1]
    all_ref[:rows, :] = sum_of([ref[...].astype(F32) for ref in up_refs]).astype(BF16)
    out = sum_of([ref[...].astype(F32) for ref in out_refs]).astype(BF16)
    all_ref[rows : rows + half, :lanes] = out[:half]
    all_ref[rows : rows + half, lanes : 2 * lanes] = out[half : 2 * half]
    all_ref[rows + half :, :lanes] = out[2 * half :]
    all_ref[rows + half :, lanes:] = jnp.zeros((16, width - lanes), BF16)


def rest_sum(ups, outs, after=()):
    n = len(ups)
    rows, width = ups[0].shape
    shape = (rows + (outs[0].shape[0] - 16) // 2 + 16, width)
    return call(
        functools.partial(rest_kernel, n), jax.ShapeDtypeStruct(shape, BF16), n_in=2 * n
    , after=after)(*ups, *outs)


def rest_pick_kernel(
    scal_ref, sum_ref, third_ref, up_ref, out_ref, gain_ref, shift_ref, unit_ref
):
    middle = (scal_ref[3] == 1) | (scal_ref[3] == 2)
    rows, width = up_ref.shape
    half, lanes = out_ref.shape[0] // 2, out_ref.shape[1]

    def fill(ref):
        up_ref[...] = ref[:rows, :].astype(F32)
        out_ref[:half, :] = ref[rows : rows + half, :lanes].astype(F32)
        out_ref[half:, :] = ref[rows : rows + half, lanes : 2 * lanes].astype(F32)
        small = ref[rows + half :, :lanes].astype(F32)
        gain_ref[0:1, :] = small[0:1]
        gain_ref[1:2, :] = small[3:4]
        shift_ref[0:2, :] = small[1:3]
        shift_ref[2:4, :] = small[4:6]
        unit_ref[...] = small[6:7]

    pl.when(middle)(lambda: fill(sum_ref))
    pl.when(jnp.logical_not(middle))(lambda: fill(third_ref))


def rest_pick(scal, total, arrived, rows, out_shape, after):
    width = total.shape[1]
    if lax.axis_size("ctx") != 4:
        arrived = total
    return call(
        rest_pick_kernel,
        (
            jax.ShapeDtypeStruct((rows, width), F32),
            jax.ShapeDtypeStruct(out_shape, F32),
            jax.ShapeDtypeStruct((2, rows), F32),
            jax.ShapeDtypeStruct((4, rows), F32),
            jax.ShapeDtypeStruct((1, rows), F32),
        ),
        smem=1,
        n_in=3,
        after=after,
    )(scal, total, arrived)


def line_pick(value, arrived):
    if lax.axis_size("ctx") != 4:
        return value
    return jnp.where(is_middle(), value, arrived)


def rotate_out(blocks):
    n = lax.axis_size("ctx")
    return [blocks[0]] + [
        lax.ppermute(blocks[d], "ctx", [(i, (i + d) % n) for i in range(n)]) for d in range(1, n)
    ]


def grad_blocks_kernel(n, axis, n_left, n_right, *refs):
    lefts, rights = refs[:n_left], refs[n_left : n_left + n_right]
    outs = refs[n_left + n_right :]
    rows = min(ref.shape[0] for ref in refs[: n_left + n_right])

    def piece(group, h, cut):
        if len(group) == 1:
            return group[0][h * rows : (h + 1) * rows, cut]
        return group[h][:, cut]

    size = (lefts, rights)[axis][0].shape[1] // n
    for d in range(n):
        cuts = [slice(None), slice(None)]
        cuts[axis] = slice(d * size, (d + 1) * size)
        outs[d][...] = sum_of(
            [mm(piece(lefts, h, cuts[0]), piece(rights, h, cuts[1]), TN) for h in range(2)]
        ).astype(BF16)


def grad_blocks(lefts, rights, n, axis):
    shape = [lefts[0].shape[1], rights[0].shape[1]]
    shape[axis] //= n
    return call(
        functools.partial(grad_blocks_kernel, n, axis, len(lefts), len(rights)),
        [jax.ShapeDtypeStruct(tuple(shape), BF16)] * n,
        n_in=len(lefts) + len(rights),
    )(*lefts, *rights)


def rotate_all(block):
    return rotate_out([block] * lax.axis_size("ctx"))


def rotate_back(blocks):
    n = lax.axis_size("ctx")
    return [blocks[0]] + [
        lax.ppermute(blocks[d], "ctx", [(i, (i - d) % n) for i in range(n)]) for d in range(1, n)
    ]


def tp_pair(own, other):
    pair = add(own, swap_core(other))
    return pair, swap_y(pair)


def share_core(own):
    return jnp.concatenate([own, swap_core(own)], axis=0)


def turn(value, axis, shift):
    size = value.shape[axis]
    doubled = jnp.concatenate([value, value], axis=axis)
    return lax.dynamic_slice_in_dim(doubled, shift, size, axis=axis)


def call(kernel, out_shape, scratch=(), smem=0, n_in=1, after=()):
    specs = [pl.BlockSpec(memory_space=pltpu.SMEM)] * smem + [
        pl.BlockSpec(memory_space=pltpu.VMEM)
    ] * (n_in - smem)
    outs = jax.tree.map(lambda _: pl.BlockSpec(memory_space=pltpu.VMEM), out_shape)

    def body(*refs):
        kernel(*refs[:n_in], *refs[n_in + len(after) :])

    def run(*args):
        return pl.pallas_call(
            body,
            out_shape=out_shape,
            in_specs=specs + [pl.BlockSpec(memory_space=pl.ANY)] * len(after),
            out_specs=outs,
            scratch_shapes=list(scratch),
            compiler_params=pltpu.CompilerParams(vmem_limit_bytes=VMEM_LIMIT),
            cost_estimate=pl.CostEstimate(flops=1000, bytes_accessed=1000, transcendentals=0),
        )(*args, *after)

    return run


def lane_low(rows):
    return lax.broadcasted_iota(jnp.int32, (rows, 2 * HD), 1) < HD


def pack_heads(rows_value, heads_ref, base, length):
    low = lane_low(length)
    for tile in range(rows_value.shape[1] // (2 * HD)):
        a = rows_value[:length, tile * 128 : tile * 128 + 128]
        b = rows_value[length:, tile * 128 : tile * 128 + 128]
        even = jnp.where(low, a, pltpu.roll(b, HD, 1))
        odd = jnp.where(low, pltpu.roll(a, HD, 1), b)
        heads_ref[2 * tile, base : base + length, :] = even.astype(BF16)
        heads_ref[2 * tile + 1, base : base + length, :] = odd.astype(BF16)


def unpack_heads(heads_ref, base, length, tile):
    low = lane_low(length)
    even = heads_ref[2 * tile, base : base + length, :].astype(F32)
    odd = heads_ref[2 * tile + 1, base : base + length, :].astype(F32)
    a = jnp.where(low, even, pltpu.roll(odd, HD, 1))
    b = jnp.where(low, pltpu.roll(even, HD, 1), odd)
    return a, b


def turned(scal_ref, d, n):
    return lax.rem(scal_ref[3] + d, n)


def project_kernel(n_parts, n, length, *refs):
    scal_ref, x_ref, bias_ref = refs[:3]
    w_refs = refs[3 : 3 + n_parts]
    out_refs = refs[3 + n_parts : 3 + n_parts + n]
    heads_ref = refs[-1]
    block = w_refs[0].shape[0]
    cols = n * HD
    for kind in range(3):
        cut = slice(kind * cols, (kind + 1) * cols)
        acc = mm(x_ref[:, :block], w_refs[0][:, cut])
        for d in range(1, n_parts):
            acc += mm(x_ref[:, d * block : (d + 1) * block], w_refs[d][:, cut])
        if kind != 1:
            acc += bias_ref[kind // 2 : kind // 2 + 1, :]
        pack_heads(acc, heads_ref, kind * length, length)
    for d in range(n):
        out_refs[d][...] = heads_ref[turned(scal_ref, d, n)]


def project(scal, x, bias, parts, length):
    n = parts[0].shape[1] // (3 * HD)
    kernel = functools.partial(project_kernel, len(parts), n, length)
    shape = jax.ShapeDtypeStruct((3 * length, 2 * HD), BF16)
    return call(
        kernel,
        [shape] * n,
        scratch=[pltpu.VMEM((n, 3 * length, 2 * HD), BF16)],
        smem=1,
        n_in=3 + len(parts),
    )(scal, x, bias, *parts)


def assemble(refs, start, length):
    return jnp.concatenate([ref[start : start + length, :] for ref in refs], axis=0)


def masked_sides(scal_ref, slot, q, k, n):
    rows = q.shape[0]
    length = rows // n
    lane = lax.broadcasted_iota(jnp.int32, (rows, 2 * HD), 1)
    spare = HD * (1 - slot)
    mine = (lane >= slot * HD) & (lane < slot * HD + HD)
    q_side = jnp.where(mine, q.astype(F32) * (HD ** -0.5), 0.0)
    q_side = jnp.where(lane == spare, 1.0, q_side).astype(BF16)
    place = lax.broadcasted_iota(jnp.int32, (length, 2 * HD), 0) + scal_ref[2]
    place = jnp.where(place >= length, place - length, place)
    place = jnp.concatenate([place + length * turned(scal_ref, n - d, n) for d in range(n)], axis=0)
    bias = jnp.where(place < scal_ref[slot], 0.0, NEGATIVE)
    k_side = jnp.where(lane == spare, bias, k.astype(F32)).astype(BF16)
    return q_side, k_side


def attend_kernel(block, n, *refs):
    scal_ref = refs[0]
    q_val, k_val, v_val = (assemble(refs[1 : 1 + n], i * block, block) for i in range(3))
    out_refs = refs[1 + n : 1 + 2 * n]
    lse_ref, all_ref = refs[1 + 2 * n :]
    length = q_val.shape[0]
    for i, value in enumerate((q_val, k_val, v_val)):
        all_ref[i] = value
    v_t = v_val.astype(F32).T.astype(BF16)
    sides = [masked_sides(scal_ref, s, q_val, k_val, n) for s in range(2)]
    low = lax.broadcasted_iota(jnp.int32, (2 * HD, block), 0) < HD
    for i, start in enumerate(range(0, length, block)):
        results = []
        for s in range(2):
            q_side, k_side = sides[s]
            scores = mm(k_side, q_side[start : start + block], NT)
            peak = jnp.max(scores, axis=0, keepdims=True)
            weights = jnp.exp(scores - peak)
            total = jnp.sum(weights, axis=0, keepdims=True)
            res = mm(v_t, weights.astype(BF16))
            results.append(res * (1.0 / total))
            lse_ref[s : s + 1, start : start + block] = peak + jnp.log(total)
        both = jnp.where(low, results[0], results[1])
        out_refs[i][...] = both.T.astype(BF16)


def attend(scal, parts, after=()):
    n = len(parts)
    block = parts[0].shape[0] // 3
    return call(
        functools.partial(attend_kernel, block, n),
        [jax.ShapeDtypeStruct((block, 2 * HD), BF16)] * n
        + [
            jax.ShapeDtypeStruct((2, n * block), F32),
            jax.ShapeDtypeStruct((3, n * block, 2 * HD), BF16),
        ],
        smem=1,
        n_in=1 + n,
        after=after,
    )(scal, *parts)


def attend_back_kernel(block, n, *refs):
    scal_ref = refs[0]
    all_ref, lse_ref = refs[1:3]
    q_val, k_val, v_val = all_ref[0], all_ref[1], all_ref[2]
    g_val = assemble(refs[3 : 3 + n], 0, block)
    out_refs = refs[3 + n : 3 + 2 * n]
    p_ref, s_ref = refs[3 + 2 * n :]
    length = q_val.shape[0]
    scale = HD ** -0.5
    k_t = k_val.astype(F32).T.astype(BF16)
    lane = lax.broadcasted_iota(jnp.int32, (length, 2 * HD), 1)
    low_t = lax.broadcasted_iota(jnp.int32, (2 * HD, block), 0) < HD
    low = lane < HD
    keep_q = []
    keep_k = []
    keep_v = []
    for s in range(2):
        q_side, k_side = masked_sides(scal_ref, s, q_val, k_val, n)
        mine = low if s == 0 else ~low
        g_side = jnp.where(mine, g_val.astype(F32), 0.0).astype(BF16)
        grads_q = []
        for start in range(0, length, block):
            scores = mm(k_side, q_side[start : start + block], NT)
            probs = jnp.exp(scores - lse_ref[s : s + 1, start : start + block])
            grad_probs = mm(v_val, g_side[start : start + block], NT)
            delta = jnp.sum(grad_probs * probs, axis=0, keepdims=True)
            grad_scores = (probs * (grad_probs - delta)).astype(BF16)
            p_ref[:, start : start + block] = probs.astype(BF16)
            s_ref[:, start : start + block] = grad_scores
            grads_q.append(mm(k_t, grad_scores))
        keep_q.append(grads_q)
        keep_v.append(mm(p_ref[...], g_val))
        keep_k.append(mm(s_ref[...], q_val))
    grad_k = jnp.where(low, keep_k[0], keep_k[1]) * scale
    grad_v = jnp.where(low, keep_v[0], keep_v[1])
    for i in range(n):
        cut = slice(i * block, (i + 1) * block)
        both = jnp.where(low_t, keep_q[0][i], keep_q[1][i]) * scale
        out_refs[i][:block, :] = both.T.astype(BF16)
        out_refs[i][block : 2 * block, :] = grad_k[cut].astype(BF16)
        out_refs[i][2 * block :, :] = grad_v[cut].astype(BF16)


def attend_back(scal, qkv, lse, grad, after=()):
    n = len(grad)
    block = grad[0].shape[0]
    length = n * block
    return call(
        functools.partial(attend_back_kernel, block, n),
        [jax.ShapeDtypeStruct((3 * block, 2 * HD), BF16)] * n,
        scratch=[pltpu.VMEM((length, length), BF16), pltpu.VMEM((length, length), BF16)],
        smem=1,
        n_in=3 + n,
        after=after,
    )(scal, qkv, lse, *grad)


def outproj_kernel(n_parts, n, length, *refs):
    scal_ref = refs[0]
    in_refs = refs[1 : 1 + n]
    w_refs = refs[1 + n : 1 + n + n_parts]
    attn_ref, own_ref, other_ref, heads_ref = refs[1 + n + n_parts :]
    half = length // 2
    for d in range(n):
        heads_ref[turned(scal_ref, d, n)] = in_refs[d][...]
    for tile in range(n // 2):
        for s, value in enumerate(unpack_heads(heads_ref, 0, length, tile)):
            for h in range(2):
                at = h * length + s * half
                attn_ref[at : at + half, tile * 128 : tile * 128 + 128] = value[
                    h * half : (h + 1) * half
                ].astype(BF16)
    block = w_refs[0].shape[1]
    for d in range(n_parts):
        part = mm(attn_ref[...], w_refs[d][...]).astype(BF16)
        own_ref[:, d * block : (d + 1) * block] = part[:length]
        other_ref[:, d * block : (d + 1) * block] = part[length:]


def outproj(scal, heads, parts, after=()):
    n = len(heads)
    length = heads[0].shape[0]
    rows, cols = 2 * length, n * HD
    width = parts[0].shape[1] * len(parts)
    return call(
        functools.partial(outproj_kernel, len(parts), n, length),
        (
            jax.ShapeDtypeStruct((rows, cols), BF16),
            jax.ShapeDtypeStruct((length, width), BF16),
            jax.ShapeDtypeStruct((length, width), BF16),
        ),
        scratch=[pltpu.VMEM((n, length, 2 * HD), BF16)],
        smem=1,
        n_in=1 + n + len(parts),
        after=after,
    )(scal, *heads, *parts)


def grad_attn_kernel(n_parts, n, length, *refs):
    scal_ref, own_ref, other_ref = refs[:3]
    w_refs = refs[3 : 3 + n_parts]
    out_refs = refs[3 + n_parts : 3 + n_parts + n]
    heads_ref = refs[-1]
    half = length // 2
    block = w_refs[0].shape[1]
    for h, g_ref in enumerate((own_ref, other_ref)):
        acc = mm(g_ref[:, :block], w_refs[0][...], NT)
        for d in range(1, n_parts):
            acc += mm(g_ref[:, d * block : (d + 1) * block], w_refs[d][...], NT)
        pack_heads(acc, heads_ref, h * half, half)
    for d in range(n):
        out_refs[d][...] = heads_ref[turned(scal_ref, d, n)]


def grad_attn(scal, own, other, parts, length):
    n = parts[0].shape[0] // HD
    return call(
        functools.partial(grad_attn_kernel, len(parts), n, length),
        [jax.ShapeDtypeStruct((length, 2 * HD), BF16)] * n,
        scratch=[pltpu.VMEM((n, length, 2 * HD), BF16)],
        smem=1,
        n_in=3 + len(parts),
    )(scal, own, other, *parts)


def grad_token_kernel(n_parts, n, length, *refs):
    scal_ref = refs[0]
    in_refs = refs[1 : 1 + n]
    w_refs = refs[1 + n : 1 + n + n_parts]
    own_ref, other_ref, rows_ref, heads_ref = refs[1 + n + n_parts :]
    half = length // 2
    cols = n * HD
    for d in range(n):
        heads_ref[turned(scal_ref, d, n)] = in_refs[d][...]
    for kind in range(3):
        for tile in range(n // 2):
            lane = kind * cols + tile * 128
            for s, value in enumerate(unpack_heads(heads_ref, kind * length, length, tile)):
                rows_ref[s * length : (s + 1) * length, lane : lane + 128] = value.astype(BF16)
    block = w_refs[0].shape[0]
    for d in range(n_parts):
        acc = mm(rows_ref[...], w_refs[d][...], NT)
        for s in range(2):
            for h in range(2):
                at = s * length + h * half
                (own_ref, other_ref)[h][
                    s * half : (s + 1) * half, d * block : (d + 1) * block
                ] = acc[at : at + half].astype(BF16)


def grad_token(scal, heads, parts, after=()):
    n = len(heads)
    length = heads[0].shape[0] // 3
    n_parts = len(parts)
    width = parts[0].shape[0] * n_parts
    return call(
        functools.partial(grad_token_kernel, n_parts, n, length),
        (
            jax.ShapeDtypeStruct((length, width), BF16),
            jax.ShapeDtypeStruct((length, width), BF16),
        ),
        scratch=[
            pltpu.VMEM((2 * length, 3 * n * HD), BF16),
            pltpu.VMEM((n, 3 * length, 2 * HD), BF16),
        ],
        smem=1,
        n_in=1 + n + n_parts,
        after=after,
    )(scal, *heads, *parts)


def grad_project_kernel(n_f, n, length, *refs):
    scal_ref, own_ref, other_ref = refs[:3]
    in_refs = refs[3 : 3 + n]
    out_refs = refs[3 + n : 3 + n + n_f]
    half = length // 2
    low = lane_low(half)
    total = None
    sums = None
    for d in range(n):
        at = turned(scal_ref, n - d, n)
        for h, x_ref in enumerate((own_ref, other_ref)):
            dq, dk, dv = (
                in_refs[d][kind * length + h * half : kind * length + (h + 1) * half, :].astype(F32)
                for kind in range(3)
            )
            first = [
                jnp.where(low, dq, pltpu.roll(dk, HD, 1)),
                jnp.where(low, pltpu.roll(dq, HD, 1), dk),
            ]
            second = [jnp.where(low, dv, 0.0), jnp.where(low, pltpu.roll(dv, HD, 1), 0.0)]
            rows = jnp.concatenate(
                [jnp.concatenate(first, axis=0), jnp.concatenate(second, axis=0)], axis=1
            )
            add = column_sum(rows)
            term = mm(rows.T.astype(BF16), x_ref[at])
            total = term if total is None else total + term
            sums = add if sums is None else sums + add
    width = total.shape[1]
    part = width // n_f
    rows = part + 32
    low = lane_low(rows // 2)
    for d in range(n_f):
        out = out_refs[d]
        value = total[:, d * part : (d + 1) * part].T
        value = jnp.concatenate([value, jnp.broadcast_to(sums, (32, sums.shape[1]))], axis=0)
        out[:rows, :] = value[:, :128].astype(BF16)
        tail = value[:, 128:]
        out[rows:, :] = jnp.where(
            low, tail[: rows // 2], pltpu.roll(tail[rows // 2 :], HD, 1)
        ).astype(BF16)


def grad_project(scal, x_own, x_other, heads, n_f, after=()):
    n = len(heads)
    length = heads[0].shape[0] // 3
    shape = ((x_own.shape[2] // n_f + 32) * 3 // 2, 2 * HD)
    return call(
        functools.partial(grad_project_kernel, n_f, n, length),
        [jax.ShapeDtypeStruct(shape, BF16)] * n_f,
        smem=1,
        n_in=3 + n,
        after=after,
    )(scal, x_own, x_other, *heads)


def spread_heads_kernel(n, *refs):
    scal_ref = refs[0]
    in_refs = refs[1 : 1 + n]
    q_ref, k_ref, v_ref, bias_ref, heads_ref = refs[1 + n :]
    rows = heads_ref.shape[1] * 2 // 3
    part = q_ref.shape[0]
    low = lane_low(rows)
    low_half = lane_low(rows // 2)
    for d in range(n):
        heads_ref[turned(scal_ref, n - d, n)] = in_refs[d][...].astype(F32)
    for tile in range(n // 2):
        cut = slice(tile * 128, tile * 128 + 128)
        a, b = heads_ref[2 * tile, :rows, :], heads_ref[2 * tile + 1, :rows, :]
        q_val = jnp.where(low, a, pltpu.roll(b, HD, 1))
        k_val = jnp.where(low, pltpu.roll(a, HD, 1), b)
        a, b = heads_ref[2 * tile, rows:, :], heads_ref[2 * tile + 1, rows:, :]
        v_val = jnp.concatenate(
            [
                jnp.where(low_half, a, pltpu.roll(b, HD, 1)),
                jnp.where(low_half, pltpu.roll(a, HD, 1), b),
            ],
            axis=0,
        )
        q_ref[:, cut] = q_val[:part]
        k_ref[:, cut] = k_val[:part]
        v_ref[:, cut] = v_val[:part]
        bias_ref[0:1, cut] = q_val[part : part + 1]
        bias_ref[1:2, cut] = v_val[part : part + 1]


def spread_heads(scal, parts):
    n = len(parts)
    rows = parts[0].shape[0]
    shape = jax.ShapeDtypeStruct((rows * 2 // 3 - 32, n * HD), F32)
    return call(
        functools.partial(spread_heads_kernel, n),
        (shape, shape, shape, jax.ShapeDtypeStruct((2, n * HD), F32)),
        scratch=[pltpu.VMEM((n, rows, 2 * HD), F32)],
        smem=1,
        n_in=1 + n,
    )(scal, *parts)


def pieces(size, count):
    step = size // count
    return [slice(i * step, (i + 1) * step) for i in range(count)]


def mean_of(values):
    return jnp.mean(values, axis=-1, keepdims=True)


def layer_stats(values):
    shifted = values - mean_of(values)
    inverse = lax.rsqrt(mean_of(shifted * shifted) + EPSILON)
    return (shifted * inverse, inverse)


def norm_back(grad_norm, normed, inverse, gain_row):
    scaled = grad_norm * gain_row
    return inverse * (scaled - mean_of(scaled) - normed * mean_of(scaled * normed))


def column_sum(values):
    return jnp.sum(values, axis=0, keepdims=True)


def first_norm_kernel(
    x_ref, pair_ref, far_ref, gain_ref, shift_ref, mid_ref, normed_ref, inverse_ref, low_ref
):
    branch = pair_ref[...].astype(F32) + far_ref[...].astype(F32) + shift_ref[0:1, :]
    normed, inverse = layer_stats(x_ref[...].astype(F32) + branch)
    middle = normed * gain_ref[0:1, :] + shift_ref[1:2, :]
    mid_ref[...] = middle
    normed_ref[...] = normed
    inverse_ref[...] = jnp.broadcast_to(inverse, inverse_ref.shape)
    low_ref[...] = middle.astype(BF16)


def first_norm(x, pair, far, gains, shift_rows):
    full = jax.ShapeDtypeStruct(x.shape, F32)
    return call(
        first_norm_kernel,
        (
            full,
            full,
            jax.ShapeDtypeStruct((x.shape[0], 128), F32),
            jax.ShapeDtypeStruct(x.shape, BF16),
        ),
        n_in=5,
    )(x, pair, far, gains, shift_rows)


def second_norm_kernel(
    mid_ref, pair_ref, far_ref, gain_ref, shift_ref, cot_ref, out_ref, grad_ref, low_ref, sum_ref
):
    mlp = pair_ref[...].astype(F32) + far_ref[...].astype(F32) + shift_ref[2:3, :]
    normed, inverse = layer_stats(mid_ref[...] + mlp)
    out_ref[...] = (normed * gain_ref[1:2, :] + shift_ref[3:4, :]).astype(BF16)
    cot = cot_ref[...].astype(F32)
    grad = norm_back(cot, normed, inverse, gain_ref[1:2, :])
    grad_ref[...] = grad
    low_ref[...] = grad.astype(BF16)
    sum_ref[0:1, :] = column_sum(cot * normed)
    sum_ref[1:2, :] = column_sum(grad)
    sum_ref[2:3, :] = column_sum(cot)


def second_norm(mid, pair, far, gains, shift_rows, cot):
    low = jax.ShapeDtypeStruct(mid.shape, BF16)
    return call(
        second_norm_kernel,
        (
            low,
            jax.ShapeDtypeStruct(mid.shape, F32),
            low,
            jax.ShapeDtypeStruct((3, mid.shape[1]), F32),
        ),
        n_in=6,
    )(mid, pair, far, gains, shift_rows, cot)


def first_back_kernel(
    two_ref, pair_ref, far_ref, normed_ref, inverse_ref, gain_ref, grad_ref, low_ref, sum_ref
):
    grad_mid = two_ref[...] + (pair_ref[...].astype(F32) + far_ref[...].astype(F32))
    normed = normed_ref[...]
    grad = norm_back(grad_mid, normed, inverse_ref[:, 0:1], gain_ref[0:1, :])
    grad_ref[...] = grad
    low_ref[...] = grad.astype(BF16)
    sum_ref[0:1, :] = column_sum(grad_mid * normed)
    sum_ref[1:2, :] = column_sum(grad)
    sum_ref[2:3, :] = column_sum(grad_mid)


def first_back(two, pair, far, normed, inverse, gains, after=()):
    return call(
        first_back_kernel,
        (
            jax.ShapeDtypeStruct(two.shape, F32),
            jax.ShapeDtypeStruct(two.shape, BF16),
            jax.ShapeDtypeStruct((3, two.shape[1]), F32),
        ),
        n_in=6,
        after=after,
    )(two, pair, far, normed, inverse, gains)


def last_sum_kernel(one_ref, pair_ref, far_ref, out_ref):
    total = pair_ref[...].astype(F32) + far_ref[...].astype(F32)
    out_ref[...] = (one_ref[...] + total).astype(BF16)


def row_cuts(refs):
    cuts = []
    start = 0
    for ref in refs:
        cuts.append((slice(start, start + ref.shape[0]), ref))
        start += ref.shape[0]
    return cuts


def column_groups(refs):
    groups = []
    column = 0
    for group in (refs[:1], refs[1:]):
        if group:
            width = group[0].shape[1]
            groups.append((slice(column, column + width), row_cuts(group)))
            column += width
    return groups


def sum_of(terms):
    total = terms[0]
    for term in terms[1:]:
        total = total + term
    return total


def feed_kernel(n_parts, *refs):
    own_ref, other_ref, bias_ref = refs[:3]
    ups = row_cuts(refs[3 : 3 + n_parts])
    downs = column_groups(refs[3 + n_parts : 3 + 2 * n_parts])
    pre_ref, act_ref, part_refs = refs[3 + 2 * n_parts], refs[4 + 2 * n_parts], refs[-2:]
    rows = own_ref.shape[0]
    for h, in_ref in enumerate((own_ref, other_ref)):
        pre = sum_of([mm(in_ref[:, cut], ref[...]) for cut, ref in ups]) + bias_ref[...]
        act = gelu_value(pre).astype(BF16)
        pre_ref[h * rows : (h + 1) * rows, :] = pre
        act_ref[h * rows : (h + 1) * rows, :] = act
        for columns, pieces in downs:
            part = sum_of([mm(act[:, cut], ref[...]) for cut, ref in pieces])
            part_refs[h][:, columns] = part.astype(BF16)


def feed(own, other, bias, ups, downs):
    rows, width = own.shape
    units = bias.shape[1]
    part = jax.ShapeDtypeStruct((rows, width), BF16)
    return call(
        functools.partial(feed_kernel, len(ups)),
        (
            jax.ShapeDtypeStruct((2 * rows, units), F32),
            jax.ShapeDtypeStruct((2 * rows, units), BF16),
            part,
            part,
        ),
        n_in=3 + 2 * len(ups),
    )(own, other, bias, *ups, *downs)


def feed_back_kernel(n_parts, *refs):
    own_ref, other_ref, pre_ref = refs[:3]
    ups = row_cuts(refs[3 : 3 + n_parts])
    downs = column_groups(refs[3 + n_parts : 3 + 2 * n_parts])
    low_ref, sum_ref, part_refs = refs[3 + 2 * n_parts], refs[4 + 2 * n_parts], refs[-2:]
    rows = own_ref.shape[0]
    sums = []
    for h, in_ref in enumerate((own_ref, other_ref)):
        terms = []
        for columns, pieces in downs:
            grads = [mm(in_ref[:, columns], ref[...], NT) for _, ref in pieces]
            terms.append(grads[0] if len(grads) == 1 else jnp.concatenate(grads, axis=1))
        grad = sum_of(terms)
        low = (grad * gelu_slope(pre_ref[h * rows : (h + 1) * rows, :])).astype(BF16)
        low_ref[h * rows : (h + 1) * rows, :] = low
        sums.append(column_sum(low.astype(F32)))
        for cut, ref in ups:
            part_refs[h][:, cut] = mm(low, ref[...], NT).astype(BF16)
    sum_ref[...] = sums[0] + sums[1]


def feed_back(own, other, pre, ups, downs, after=()):
    rows, width = own.shape
    units = pre.shape[1]
    part = jax.ShapeDtypeStruct((rows, width), BF16)
    return call(
        functools.partial(feed_back_kernel, len(ups)),
        (
            jax.ShapeDtypeStruct((2 * rows, units), BF16),
            jax.ShapeDtypeStruct((1, units), F32),
            part,
            part,
        ),
        n_in=3 + 2 * len(ups),
        after=after,
    )(own, other, pre, *ups, *downs)


def gelu_value(values):
    return 0.5 * values * (1.0 + lax.erf(values * 0.7071067811865476))


def gelu_slope(values):
    return (
        0.5 * (1.0 + lax.erf(values * 0.7071067811865476))
        + values * jnp.exp(-0.5 * values * values) * 0.3989422804014327
    )


def on_device(
    hidden, lengths, w_qkv, b_qkv, w_out, norm_gain, shifts, up_weight, b_up, down_weight, cotangent
):
    sequences, local_len, width = hidden.shape
    half = local_len // 2
    rows = sequences * local_len
    own_rows = rows // 2
    n_f = lax.axis_size("fsdp")
    part = width // n_f
    cols = w_qkv.shape[2]
    f_at = lax.axis_index("fsdp")
    core = lax.axis_index("tp") % 2

    def localise(value):
        value = turn(value, 2, f_at * part)
        value = turn(value, 1, core * half)
        return value

    x_slots = localise(hidden)
    x_rows = x_slots.reshape(rows, width)
    x_own = x_slots[:, :half].reshape(own_rows, width)
    cot_own = localise(cotangent)[:, :half].reshape(own_rows, width)

    w_parts = few(gather_parts(w_qkv.reshape(part, 3 * cols)), 0)
    norm_gain, shifts, b_qkv, b_up, w_out, ups, downs, _ = tie(
        norm_gain,
        shifts,
        b_qkv,
        b_up,
        w_out,
        split_rows(up_weight),
        split_rows(down_weight),
        x_own,
    )
    bias_len = b_qkv.shape[2]
    unit_len = b_up.shape[1]
    vectors = jnp.concatenate(
        [norm_gain.reshape(-1), shifts.reshape(-1), b_qkv.reshape(-1), b_up.reshape(-1)]
    ).reshape(1, -1)
    vectors = jnp.concatenate(gather_parts(vectors), axis=0)
    cuts = [2 * part, 6 * part, 6 * part + 2 * bias_len]
    gains = vectors[:, : cuts[0]].reshape(n_f, 2, part).transpose(1, 0, 2).reshape(2, width)
    shift_rows = vectors[:, cuts[0] : cuts[1]].reshape(n_f, 4, part).transpose(1, 0, 2)
    shift_rows = shift_rows.reshape(4, width).astype(F32)
    gains = gains.astype(F32)
    back = (n_f - f_at) % n_f
    b_pair = vectors[:, cuts[1] : cuts[2]].reshape(n_f, 2, bias_len).transpose(1, 0, 2)
    b_pair = turn(b_pair, 1, back).reshape(2, cols).astype(F32)
    up_bias = turn(vectors[:, cuts[2] :], 0, back).reshape(1, n_f * unit_len).astype(F32)
    w_out_parts = few(gather_parts(w_out), 1)
    up_pieces = split_gather(up_weight, ups, 0)
    down_pieces = split_gather(down_weight, downs, 1)

    scal = jnp.concatenate(
        [
            lengths,
            (core * half).astype(jnp.int32).reshape(1),
            lax.axis_index("ctx").astype(jnp.int32).reshape(1),
        ]
    )
    heads = rotate_out(project(scal, x_rows, b_pair, w_parts, local_len))
    *attn_parts, lse, qkv_all = attend(scal, heads, after=up_pieces[1:2])
    x_gather, _ = tie(x_own, lse)
    x_all_own = lax.all_gather(x_gather, "ctx", axis=0)
    x_all_other = swap_core(x_all_own)
    attn_rows, own, other = outproj(
        scal, rotate_back(attn_parts), w_out_parts, after=up_pieces[2:] + down_pieces[1:2]
    )

    pair = add(own, swap_core(other), after=down_pieces[2:])
    far = swap_y(pair)
    middle, normed_one, inverse_one, mid_own = first_norm(
        x_own, pair, far, gains, shift_rows
    )
    mid_other = swap_core(mid_own)
    pre_act, act_low, *partial = feed(mid_own, mid_other, up_bias, up_pieces, down_pieces)

    result_own, grad_two, two_own, two_sums = second_norm(
        middle, *tp_pair(*partial), gains, shift_rows, cot_own
    )
    two_other = swap_core(two_own)
    down_blocks = grad_blocks([act_low], [two_own, two_other], n_f, 1)
    pre_low, unit_sums, *partial = feed_back(
        two_own, two_other, pre_act, up_pieces, down_pieces, after=down_blocks[:1]
    )
    down_blocks = scatter_start(down_blocks)
    pair, far = tp_pair(*partial)
    up_blocks = grad_blocks([mid_own, mid_other], [pre_low], n_f, 0)

    grad_one, one_own, one_sums = first_back(
        grad_two, pair, far, normed_one, inverse_one, gains, after=up_blocks[:1]
    )
    up_blocks = scatter_start(up_blocks)
    one_other = swap_core(one_own)
    norm_sums = jnp.concatenate([one_sums, two_sums], axis=0)
    unit_sums = turn(unit_sums, 1, f_at * unit_len)
    grad_parts = grad_attn(scal, one_own, one_other, w_out_parts, local_len)

    grad_heads = rotate_out(grad_parts)
    down_sum = add(*down_blocks, after=grad_heads[1:])
    down_step = line_first(down_sum)
    head_grads = attend_back(
        scal, qkv_all, lse, grad_heads, after=[down_sum, x_all_other]
    )

    out_blocks = scatter_start(
        out_gradient(
            attn_rows, one_own, one_other, norm_sums, swap_core(norm_sums), unit_sums, n_f,
            after=head_grads[:1],
        )
    )
    head_rows = rotate_back(head_grads)
    rest = rest_sum(up_blocks, out_blocks, after=head_rows[1:])
    rest_step = line_first(rest)
    down_sum = line_add(down_sum, down_step, after=head_rows[1:])
    down_step = line_second(down_sum)

    next_rest = line_add(rest, rest_step, after=[down_step])
    down_sum = line_add(down_sum, down_step, after=[rest_step])
    rest, rest_step = next_rest, line_second(next_rest)
    down_step = line_third(down_sum)
    qkv_blocks = scatter_start(
        grad_project(scal, x_all_own, x_all_other, head_grads, n_f, after=[rest])
    )
    qkv_parts = rotate_all(add(*qkv_blocks))
    own, other = grad_token(scal, head_rows, w_parts, after=[rest])
    other = swap_core(other)

    rest = line_add(rest, rest_step, after=[down_step] + qkv_parts[1:])
    rest_step = line_third(rest)
    pair = add(own, other, after=[rest])
    far = swap_y(pair)
    grad_tokens = call(last_sum_kernel, jax.ShapeDtypeStruct(one_own.shape, BF16), n_in=3)(
        grad_one, pair, far
    )
    grad_q, grad_k, grad_v, grad_bias = spread_heads(scal, qkv_parts)
    grad_qkv = jnp.stack([grad_q, grad_k, grad_v], axis=1)
    grad_bias = lax.dynamic_slice_in_dim(grad_bias, f_at * bias_len, bias_len, axis=1)
    grad_bias = grad_bias.reshape(b_qkv.shape)

    grad_down = line_pick(down_sum, down_step).astype(F32)

    def restore(own):
        both = share_core(own).reshape(2, sequences, half, width)
        both = turn(both, 0, core).transpose(1, 0, 2, 3).reshape(sequences, local_len, width)
        return turn(both, 2, ((n_f - f_at) % n_f) * part)

    result = restore(result_own)
    grad_up, grad_out, grad_gain, grad_shift, grad_unit = rest_pick(
        scal, rest, rest_step, part, w_out.shape, after=[result, grad_qkv, grad_down]
    )
    return (
        result,
        restore(grad_tokens),
        grad_qkv,
        grad_bias,
        grad_out,
        grad_gain,
        grad_shift,
        grad_up,
        grad_unit.reshape(b_up.shape),
        grad_down,
    )


def solution(mesh):
    in_specs = (
        P("fsdp", "ctx", None),
        P("fsdp"),
        P("fsdp", None, "tp"),
        P(None, "tp", "fsdp"),
        P("tp", "fsdp"),
        P(None, "fsdp"),
        P(None, "fsdp"),
        P("fsdp", "tp"),
        P("tp", "fsdp"),
        P("tp", "fsdp"),
        P("fsdp", "ctx", None),
    )
    out_specs = (
        P("fsdp", "ctx", None),
        P("fsdp", "ctx", None),
        P("fsdp", None, "tp"),
        P(None, "tp", "fsdp"),
        P("tp", "fsdp"),
        P(None, "fsdp"),
        P(None, "fsdp"),
        P("fsdp", "tp"),
        P("tp", "fsdp"),
        P("tp", "fsdp"),
    )
    return jax.shard_map(
        on_device, mesh=mesh, in_specs=in_specs, out_specs=out_specs, check_vma=False
    )
```

```python
import functools

import jax
import jax.numpy as jnp
from jax import lax
from jax.experimental import pallas as pl
from jax.experimental.pallas import tpu as pltpu
from jax.sharding import PartitionSpec as P

HD = 64
EPSILON = 1e-12
NEGATIVE = -1e30
F32 = jnp.float32
BF16 = jnp.bfloat16
VMEM_LIMIT = 32 * 1024 * 1024

NT = (((1,), (1,)), ((), ()))
TN = (((0,), (0,)), ((), ()))
NN = (((1,), (0,)), ((), ()))


def mm(a, b, dims=NN):
    return lax.dot_general(a, b, dims, preferred_element_type=F32)


def swap_core(value):
    n = lax.axis_size("tp")
    return lax.ppermute(value, "tp", [(i, i ^ 1) for i in range(n)])


def swap_y(value):
    n = lax.axis_size("tp")
    return lax.ppermute(value, "tp", [(i, i ^ 2) for i in range(n)])


def gather_parts(value):
    n = lax.axis_size("fsdp")
    parts = [value]
    for d in range(1, n):
        parts.append(lax.ppermute(value, "fsdp", [((i + d) % n, i) for i in range(n)]))
    return parts


def split_rows(value):
    if lax.axis_size("fsdp") != 2:
        return [value]
    rows = value.shape[0] // 2
    return [value[:rows], value[rows:]]


def split_gather(value, pieces, axis):
    if len(pieces) == 1:
        return few(gather_parts(pieces[0]), axis)
    return [value] + [gather_parts(piece)[1] for piece in pieces]


def few(parts, axis):
    return parts if len(parts) == 2 else [jnp.concatenate(parts, axis=axis)]


def scatter_start(blocks):
    n = lax.axis_size("fsdp")
    return [blocks[0]] + [
        lax.ppermute(blocks[d], "fsdp", [(i, (i + d) % n) for i in range(n)]) for d in range(1, n)
    ]


def add_kernel(*refs):
    total = refs[0][...].astype(F32)
    for ref in refs[1:-1]:
        total = total + ref[...].astype(F32)
    refs[-1][...] = total.astype(BF16)


def add(*values, after=()):
    shape = jax.ShapeDtypeStruct(values[0].shape, BF16)
    return call(add_kernel, shape, n_in=len(values), after=after)(*values)


def tie(*values):
    return lax.optimization_barrier(values)


def is_middle():
    place = lax.axis_index("ctx")
    return (place == 1) | (place == 2)


def line_first(value):
    if lax.axis_size("ctx") != 4:
        return value
    return lax.ppermute(value, "ctx", [(0, 1), (3, 2)])


def line_second(value):
    if lax.axis_size("ctx") != 4:
        return lax.psum(value, "ctx")
    return lax.ppermute(value, "ctx", [(1, 2), (2, 1)])


def line_third(value):
    if lax.axis_size("ctx") != 4:
        return value
    return lax.ppermute(value, "ctx", [(1, 0), (2, 3)])


def line_add(value, arrived, after=()):
    if lax.axis_size("ctx") != 4:
        return arrived
    return add(value, arrived, after=after)


def out_blocks_kernel(n, attn_ref, own_ref, other_ref, sums_ref, far_sums_ref, unit_ref, *outs):
    half = own_ref.shape[0]
    rows = attn_ref.shape[1]
    sums = sums_ref[...] + far_sums_ref[...]
    width = sums.shape[1]
    sums = jnp.concatenate(
        [sums, unit_ref[...], jnp.zeros((15 - sums.shape[0], width), F32)], axis=0
    ).astype(BF16)
    size = width // n
    for d in range(n):
        cut = slice(d * size, (d + 1) * size)
        total = mm(attn_ref[:half, :], own_ref[:, cut], TN)
        total += mm(attn_ref[half:, :], other_ref[:, cut], TN)
        outs[d][:rows, :] = total.astype(BF16)
        outs[d][rows:, :] = sums[:, cut]


def out_gradient(attn, own, other, sums, far_sums, units, n, after):
    shape = (attn.shape[1] + 16, own.shape[1] // n)
    return call(
        functools.partial(out_blocks_kernel, n),
        [jax.ShapeDtypeStruct(shape, BF16)] * n,
        n_in=6,
        after=after,
    )(attn, own, other, sums, far_sums, units)


def rest_kernel(n, *refs):
    up_refs, out_refs = refs[:n], refs[n : 2 * n]
    all_ref = refs[2 * n]
    rows, width = up_refs[0].shape
    half, lanes = (out_refs[0].shape[0] - 16) // 2, out_refs[0].shape[1]
    all_ref[:rows, :] = sum_of([ref[...].astype(F32) for ref in up_refs]).astype(BF16)
    out = sum_of([ref[...].astype(F32) for ref in out_refs]).astype(BF16)
    all_ref[rows : rows + half, :lanes] = out[:half]
    all_ref[rows : rows + half, lanes : 2 * lanes] = out[half : 2 * half]
    all_ref[rows + half :, :lanes] = out[2 * half :]
    all_ref[rows + half :, lanes:] = jnp.zeros((16, width - lanes), BF16)


def rest_sum(ups, outs, after=()):
    n = len(ups)
    rows, width = ups[0].shape
    shape = (rows + (outs[0].shape[0] - 16) // 2 + 16, width)
    return call(
        functools.partial(rest_kernel, n), jax.ShapeDtypeStruct(shape, BF16), n_in=2 * n
    , after=after)(*ups, *outs)


def rest_pick_kernel(
    scal_ref, sum_ref, third_ref, up_ref, out_ref, gain_ref, shift_ref, unit_ref
):
    middle = (scal_ref[3] == 1) | (scal_ref[3] == 2)
    rows, width = up_ref.shape
    half, lanes = out_ref.shape[0] // 2, out_ref.shape[1]

    def fill(ref):
        up_ref[...] = ref[:rows, :].astype(F32)
        out_ref[:half, :] = ref[rows : rows + half, :lanes].astype(F32)
        out_ref[half:, :] = ref[rows : rows + half, lanes : 2 * lanes].astype(F32)
        small = ref[rows + half :, :lanes].astype(F32)
        gain_ref[0:1, :] = small[0:1]
        gain_ref[1:2, :] = small[3:4]
        shift_ref[0:2, :] = small[1:3]
        shift_ref[2:4, :] = small[4:6]
        unit_ref[...] = small[6:7]

    pl.when(middle)(lambda: fill(sum_ref))
    pl.when(jnp.logical_not(middle))(lambda: fill(third_ref))


def rest_pick(scal, total, arrived, rows, out_shape, after):
    width = total.shape[1]
    if lax.axis_size("ctx") != 4:
        arrived = total
    return call(
        rest_pick_kernel,
        (
            jax.ShapeDtypeStruct((rows, width), F32),
            jax.ShapeDtypeStruct(out_shape, F32),
            jax.ShapeDtypeStruct((2, rows), F32),
            jax.ShapeDtypeStruct((4, rows), F32),
            jax.ShapeDtypeStruct((1, rows), F32),
        ),
        smem=1,
        n_in=3,
        after=after,
    )(scal, total, arrived)


def line_pick(value, arrived):
    if lax.axis_size("ctx") != 4:
        return value
    return jnp.where(is_middle(), value, arrived)


def rotate_out(blocks):
    n = lax.axis_size("ctx")
    return [blocks[0]] + [
        lax.ppermute(blocks[d], "ctx", [(i, (i + d) % n) for i in range(n)]) for d in range(1, n)
    ]


def grad_blocks_kernel(n, axis, n_left, n_right, *refs):
    lefts, rights = refs[:n_left], refs[n_left : n_left + n_right]
    outs = refs[n_left + n_right :]
    rows = min(ref.shape[0] for ref in refs[: n_left + n_right])

    def piece(group, h, cut):
        if len(group) == 1:
            return group[0][h * rows : (h + 1) * rows, cut]
        return group[h][:, cut]

    size = (lefts, rights)[axis][0].shape[1] // n
    for d in range(n):
        cuts = [slice(None), slice(None)]
        cuts[axis] = slice(d * size, (d + 1) * size)
        outs[d][...] = sum_of(
            [mm(piece(lefts, h, cuts[0]), piece(rights, h, cuts[1]), TN) for h in range(2)]
        ).astype(BF16)


def grad_blocks(lefts, rights, n, axis):
    shape = [lefts[0].shape[1], rights[0].shape[1]]
    shape[axis] //= n
    return call(
        functools.partial(grad_blocks_kernel, n, axis, len(lefts), len(rights)),
        [jax.ShapeDtypeStruct(tuple(shape), BF16)] * n,
        n_in=len(lefts) + len(rights),
    )(*lefts, *rights)


def rotate_all(block):
    return rotate_out([block] * lax.axis_size("ctx"))


def rotate_back(blocks):
    n = lax.axis_size("ctx")
    return [blocks[0]] + [
        lax.ppermute(blocks[d], "ctx", [(i, (i - d) % n) for i in range(n)]) for d in range(1, n)
    ]


def tp_pair(own, other):
    pair = add(own, swap_core(other))
    return pair, swap_y(pair)


def share_core(own):
    return jnp.concatenate([own, swap_core(own)], axis=0)


def turn(value, axis, shift):
    size = value.shape[axis]
    doubled = jnp.concatenate([value, value], axis=axis)
    return lax.dynamic_slice_in_dim(doubled, shift, size, axis=axis)


def call(kernel, out_shape, scratch=(), smem=0, n_in=1, after=()):
    specs = [pl.BlockSpec(memory_space=pltpu.SMEM)] * smem + [
        pl.BlockSpec(memory_space=pltpu.VMEM)
    ] * (n_in - smem)
    outs = jax.tree.map(lambda _: pl.BlockSpec(memory_space=pltpu.VMEM), out_shape)

    def body(*refs):
        kernel(*refs[:n_in], *refs[n_in + len(after) :])

    def run(*args):
        return pl.pallas_call(
            body,
            out_shape=out_shape,
            in_specs=specs + [pl.BlockSpec(memory_space=pl.ANY)] * len(after),
            out_specs=outs,
            scratch_shapes=list(scratch),
            compiler_params=pltpu.CompilerParams(vmem_limit_bytes=VMEM_LIMIT),
            cost_estimate=pl.CostEstimate(flops=1000, bytes_accessed=1000, transcendentals=0),
        )(*args, *after)

    return run


def lane_low(rows):
    return lax.broadcasted_iota(jnp.int32, (rows, 2 * HD), 1) < HD


def pack_heads(rows_value, heads_ref, base, length):
    low = lane_low(length)
    for tile in range(rows_value.shape[1] // (2 * HD)):
        a = rows_value[:length, tile * 128 : tile * 128 + 128]
        b = rows_value[length:, tile * 128 : tile * 128 + 128]
        even = jnp.where(low, a, pltpu.roll(b, HD, 1))
        odd = jnp.where(low, pltpu.roll(a, HD, 1), b)
        heads_ref[2 * tile, base : base + length, :] = even.astype(BF16)
        heads_ref[2 * tile + 1, base : base + length, :] = odd.astype(BF16)


def unpack_heads(heads_ref, base, length, tile):
    low = lane_low(length)
    even = heads_ref[2 * tile, base : base + length, :].astype(F32)
    odd = heads_ref[2 * tile + 1, base : base + length, :].astype(F32)
    a = jnp.where(low, even, pltpu.roll(odd, HD, 1))
    b = jnp.where(low, pltpu.roll(even, HD, 1), odd)
    return a, b


def turned(scal_ref, d, n):
    return lax.rem(scal_ref[3] + d, n)


def project_kernel(n_parts, n, length, *refs):
    scal_ref, x_ref, bias_ref = refs[:3]
    w_refs = refs[3 : 3 + n_parts]
    out_refs = refs[3 + n_parts : 3 + n_parts + n]
    heads_ref = refs[-1]
    block = w_refs[0].shape[0]
    cols = n * HD
    for kind in range(3):
        cut = slice(kind * cols, (kind + 1) * cols)
        acc = mm(x_ref[:, :block], w_refs[0][:, cut])
        for d in range(1, n_parts):
            acc += mm(x_ref[:, d * block : (d + 1) * block], w_refs[d][:, cut])
        if kind != 1:
            acc += bias_ref[kind // 2 : kind // 2 + 1, :]
        pack_heads(acc, heads_ref, kind * length, length)
    for d in range(n):
        out_refs[d][...] = heads_ref[turned(scal_ref, d, n)]


def project(scal, x, bias, parts, length):
    n = parts[0].shape[1] // (3 * HD)
    kernel = functools.partial(project_kernel, len(parts), n, length)
    shape = jax.ShapeDtypeStruct((3 * length, 2 * HD), BF16)
    return call(
        kernel,
        [shape] * n,
        scratch=[pltpu.VMEM((n, 3 * length, 2 * HD), BF16)],
        smem=1,
        n_in=3 + len(parts),
    )(scal, x, bias, *parts)


def assemble(refs, start, length):
    return jnp.concatenate([ref[start : start + length, :] for ref in refs], axis=0)


def masked_sides(scal_ref, slot, q, k, n):
    rows = q.shape[0]
    length = rows // n
    lane = lax.broadcasted_iota(jnp.int32, (rows, 2 * HD), 1)
    spare = HD * (1 - slot)
    mine = (lane >= slot * HD) & (lane < slot * HD + HD)
    q_side = jnp.where(mine, q.astype(F32) * (HD ** -0.5), 0.0)
    q_side = jnp.where(lane == spare, 1.0, q_side).astype(BF16)
    place = lax.broadcasted_iota(jnp.int32, (length, 2 * HD), 0) + scal_ref[2]
    place = jnp.where(place >= length, place - length, place)
    place = jnp.concatenate([place + length * turned(scal_ref, n - d, n) for d in range(n)], axis=0)
    bias = jnp.where(place < scal_ref[slot], 0.0, NEGATIVE)
    k_side = jnp.where(lane == spare, bias, k.astype(F32)).astype(BF16)
    return q_side, k_side


def attend_kernel(block, n, *refs):
    scal_ref = refs[0]
    q_val, k_val, v_val = (assemble(refs[1 : 1 + n], i * block, block) for i in range(3))
    out_refs = refs[1 + n : 1 + 2 * n]
    lse_ref, all_ref = refs[1 + 2 * n :]
    length = q_val.shape[0]
    for i, value in enumerate((q_val, k_val, v_val)):
        all_ref[i] = value
    v_t = v_val.astype(F32).T.astype(BF16)
    sides = [masked_sides(scal_ref, s, q_val, k_val, n) for s in range(2)]
    low = lax.broadcasted_iota(jnp.int32, (2 * HD, block), 0) < HD
    for i, start in enumerate(range(0, length, block)):
        results = []
        for s in range(2):
            q_side, k_side = sides[s]
            pieces = []
            for at in range(start, start + block, 128):
                scores = mm(k_side, q_side[at : at + 128], NT)
                peak = jnp.max(scores, axis=0, keepdims=True)
                weights = jnp.exp(scores - peak)
                total = jnp.sum(weights, axis=0, keepdims=True)
                res = mm(v_t, weights.astype(BF16))
                pieces.append(res * (1.0 / total))
                lse_ref[s : s + 1, at : at + 128] = peak + jnp.log(total)
            results.append(jnp.concatenate(pieces, axis=1))
        both = jnp.where(low, results[0], results[1])
        out_refs[i][...] = both.T.astype(BF16)


def attend(scal, parts, after=()):
    n = len(parts)
    block = parts[0].shape[0] // 3
    return call(
        functools.partial(attend_kernel, block, n),
        [jax.ShapeDtypeStruct((block, 2 * HD), BF16)] * n
        + [
            jax.ShapeDtypeStruct((2, n * block), F32),
            jax.ShapeDtypeStruct((3, n * block, 2 * HD), BF16),
        ],
        smem=1,
        n_in=1 + n,
        after=after,
    )(scal, *parts)


def attend_back_kernel(block, n, *refs):
    scal_ref = refs[0]
    all_ref, lse_ref = refs[1:3]
    q_val, k_val, v_val = all_ref[0], all_ref[1], all_ref[2]
    g_val = assemble(refs[3 : 3 + n], 0, block)
    out_refs = refs[3 + n : 3 + 2 * n]
    p_ref, s_ref = refs[3 + 2 * n :]
    length = q_val.shape[0]
    scale = HD ** -0.5
    k_t = k_val.astype(F32).T.astype(BF16)
    lane = lax.broadcasted_iota(jnp.int32, (length, 2 * HD), 1)
    low_t = lax.broadcasted_iota(jnp.int32, (2 * HD, block), 0) < HD
    low = lane < HD
    keep_q = []
    keep_k = []
    keep_v = []
    for s in range(2):
        q_side, k_side = masked_sides(scal_ref, s, q_val, k_val, n)
        mine = low if s == 0 else ~low
        g_side = jnp.where(mine, g_val.astype(F32), 0.0).astype(BF16)
        grads_q = []
        for start in range(0, length, block):
            scores = mm(k_side, q_side[start : start + block], NT)
            probs = jnp.exp(scores - lse_ref[s : s + 1, start : start + block])
            grad_probs = mm(v_val, g_side[start : start + block], NT)
            delta = jnp.sum(grad_probs * probs, axis=0, keepdims=True)
            grad_scores = (probs * (grad_probs - delta)).astype(BF16)
            p_ref[:, start : start + block] = probs.astype(BF16)
            s_ref[:, start : start + block] = grad_scores
            grads_q.append(mm(k_t, grad_scores))
        keep_q.append(grads_q)
        keep_v.append(mm(p_ref[...], g_val))
        keep_k.append(mm(s_ref[...], q_val))
    grad_k = jnp.where(low, keep_k[0], keep_k[1]) * scale
    grad_v = jnp.where(low, keep_v[0], keep_v[1])
    for i in range(n):
        cut = slice(i * block, (i + 1) * block)
        both = jnp.where(low_t, keep_q[0][i], keep_q[1][i]) * scale
        out_refs[i][:block, :] = both.T.astype(BF16)
        out_refs[i][block : 2 * block, :] = grad_k[cut].astype(BF16)
        out_refs[i][2 * block :, :] = grad_v[cut].astype(BF16)


def attend_back(scal, qkv, lse, grad, after=()):
    n = len(grad)
    block = grad[0].shape[0]
    length = n * block
    return call(
        functools.partial(attend_back_kernel, block, n),
        [jax.ShapeDtypeStruct((3 * block, 2 * HD), BF16)] * n,
        scratch=[pltpu.VMEM((length, length), BF16), pltpu.VMEM((length, length), BF16)],
        smem=1,
        n_in=3 + n,
        after=after,
    )(scal, qkv, lse, *grad)


def outproj_kernel(n_parts, n, length, *refs):
    scal_ref = refs[0]
    in_refs = refs[1 : 1 + n]
    w_refs = refs[1 + n : 1 + n + n_parts]
    attn_ref, own_ref, other_ref, heads_ref = refs[1 + n + n_parts :]
    half = length // 2
    for d in range(n):
        heads_ref[turned(scal_ref, d, n)] = in_refs[d][...]
    for tile in range(n // 2):
        for s, value in enumerate(unpack_heads(heads_ref, 0, length, tile)):
            for h in range(2):
                at = h * length + s * half
                attn_ref[at : at + half, tile * 128 : tile * 128 + 128] = value[
                    h * half : (h + 1) * half
                ].astype(BF16)
    block = w_refs[0].shape[1]
    for d in range(n_parts):
        part = mm(attn_ref[...], w_refs[d][...]).astype(BF16)
        own_ref[:, d * block : (d + 1) * block] = part[:length]
        other_ref[:, d * block : (d + 1) * block] = part[length:]


def outproj(scal, heads, parts, after=()):
    n = len(heads)
    length = heads[0].shape[0]
    rows, cols = 2 * length, n * HD
    width = parts[0].shape[1] * len(parts)
    return call(
        functools.partial(outproj_kernel, len(parts), n, length),
        (
            jax.ShapeDtypeStruct((rows, cols), BF16),
            jax.ShapeDtypeStruct((length, width), BF16),
            jax.ShapeDtypeStruct((length, width), BF16),
        ),
        scratch=[pltpu.VMEM((n, length, 2 * HD), BF16)],
        smem=1,
        n_in=1 + n + len(parts),
        after=after,
    )(scal, *heads, *parts)


def grad_attn_kernel(n_parts, n, length, *refs):
    scal_ref, own_ref, other_ref = refs[:3]
    w_refs = refs[3 : 3 + n_parts]
    out_refs = refs[3 + n_parts : 3 + n_parts + n]
    heads_ref = refs[-1]
    half = length // 2
    block = w_refs[0].shape[1]
    for h, g_ref in enumerate((own_ref, other_ref)):
        acc = mm(g_ref[:, :block], w_refs[0][...], NT)
        for d in range(1, n_parts):
            acc += mm(g_ref[:, d * block : (d + 1) * block], w_refs[d][...], NT)
        pack_heads(acc, heads_ref, h * half, half)
    for d in range(n):
        out_refs[d][...] = heads_ref[turned(scal_ref, d, n)]


def grad_attn(scal, own, other, parts, length):
    n = parts[0].shape[0] // HD
    return call(
        functools.partial(grad_attn_kernel, len(parts), n, length),
        [jax.ShapeDtypeStruct((length, 2 * HD), BF16)] * n,
        scratch=[pltpu.VMEM((n, length, 2 * HD), BF16)],
        smem=1,
        n_in=3 + len(parts),
    )(scal, own, other, *parts)


def grad_token_kernel(n_parts, n, length, *refs):
    scal_ref = refs[0]
    in_refs = refs[1 : 1 + n]
    w_refs = refs[1 + n : 1 + n + n_parts]
    own_ref, other_ref, rows_ref, heads_ref = refs[1 + n + n_parts :]
    half = length // 2
    cols = n * HD
    for d in range(n):
        heads_ref[turned(scal_ref, d, n)] = in_refs[d][...]
    for kind in range(3):
        for tile in range(n // 2):
            lane = kind * cols + tile * 128
            for s, value in enumerate(unpack_heads(heads_ref, kind * length, length, tile)):
                rows_ref[s * length : (s + 1) * length, lane : lane + 128] = value.astype(BF16)
    block = w_refs[0].shape[0]
    for d in range(n_parts):
        acc = mm(rows_ref[...], w_refs[d][...], NT)
        for s in range(2):
            for h in range(2):
                at = s * length + h * half
                (own_ref, other_ref)[h][
                    s * half : (s + 1) * half, d * block : (d + 1) * block
                ] = acc[at : at + half].astype(BF16)


def grad_token(scal, heads, parts, after=()):
    n = len(heads)
    length = heads[0].shape[0] // 3
    n_parts = len(parts)
    width = parts[0].shape[0] * n_parts
    return call(
        functools.partial(grad_token_kernel, n_parts, n, length),
        (
            jax.ShapeDtypeStruct((length, width), BF16),
            jax.ShapeDtypeStruct((length, width), BF16),
        ),
        scratch=[
            pltpu.VMEM((2 * length, 3 * n * HD), BF16),
            pltpu.VMEM((n, 3 * length, 2 * HD), BF16),
        ],
        smem=1,
        n_in=1 + n + n_parts,
        after=after,
    )(scal, *heads, *parts)


def grad_project_kernel(n_f, n, length, *refs):
    scal_ref, own_ref, other_ref = refs[:3]
    in_refs = refs[3 : 3 + n]
    out_refs = refs[3 + n : 3 + n + n_f]
    half = length // 2
    low = lane_low(half)
    total = None
    sums = None
    for d in range(n):
        at = turned(scal_ref, n - d, n)
        for h, x_ref in enumerate((own_ref, other_ref)):
            dq, dk, dv = (
                in_refs[d][kind * length + h * half : kind * length + (h + 1) * half, :].astype(F32)
                for kind in range(3)
            )
            first = [
                jnp.where(low, dq, pltpu.roll(dk, HD, 1)),
                jnp.where(low, pltpu.roll(dq, HD, 1), dk),
            ]
            second = [jnp.where(low, dv, 0.0), jnp.where(low, pltpu.roll(dv, HD, 1), 0.0)]
            rows = jnp.concatenate(
                [jnp.concatenate(first, axis=0), jnp.concatenate(second, axis=0)], axis=1
            )
            add = column_sum(rows)
            term = mm(rows.T.astype(BF16), x_ref[at])
            total = term if total is None else total + term
            sums = add if sums is None else sums + add
    width = total.shape[1]
    part = width // n_f
    rows = part + 32
    low = lane_low(rows // 2)
    for d in range(n_f):
        out = out_refs[d]
        value = total[:, d * part : (d + 1) * part].T
        value = jnp.concatenate([value, jnp.broadcast_to(sums, (32, sums.shape[1]))], axis=0)
        out[:rows, :] = value[:, :128].astype(BF16)
        tail = value[:, 128:]
        out[rows:, :] = jnp.where(
            low, tail[: rows // 2], pltpu.roll(tail[rows // 2 :], HD, 1)
        ).astype(BF16)


def grad_project(scal, x_own, x_other, heads, n_f, after=()):
    n = len(heads)
    length = heads[0].shape[0] // 3
    shape = ((x_own.shape[2] // n_f + 32) * 3 // 2, 2 * HD)
    return call(
        functools.partial(grad_project_kernel, n_f, n, length),
        [jax.ShapeDtypeStruct(shape, BF16)] * n_f,
        smem=1,
        n_in=3 + n,
        after=after,
    )(scal, x_own, x_other, *heads)


def spread_heads_kernel(n, *refs):
    scal_ref = refs[0]
    in_refs = refs[1 : 1 + n]
    q_ref, k_ref, v_ref, bias_ref, heads_ref = refs[1 + n :]
    rows = heads_ref.shape[1] * 2 // 3
    part = q_ref.shape[0]
    low = lane_low(rows)
    low_half = lane_low(rows // 2)
    for d in range(n):
        heads_ref[turned(scal_ref, n - d, n)] = in_refs[d][...].astype(F32)
    for tile in range(n // 2):
        cut = slice(tile * 128, tile * 128 + 128)
        a, b = heads_ref[2 * tile, :rows, :], heads_ref[2 * tile + 1, :rows, :]
        q_val = jnp.where(low, a, pltpu.roll(b, HD, 1))
        k_val = jnp.where(low, pltpu.roll(a, HD, 1), b)
        a, b = heads_ref[2 * tile, rows:, :], heads_ref[2 * tile + 1, rows:, :]
        v_val = jnp.concatenate(
            [
                jnp.where(low_half, a, pltpu.roll(b, HD, 1)),
                jnp.where(low_half, pltpu.roll(a, HD, 1), b),
            ],
            axis=0,
        )
        q_ref[:, cut] = q_val[:part]
        k_ref[:, cut] = k_val[:part]
        v_ref[:, cut] = v_val[:part]
        bias_ref[0:1, cut] = q_val[part : part + 1]
        bias_ref[1:2, cut] = v_val[part : part + 1]


def spread_heads(scal, parts):
    n = len(parts)
    rows = parts[0].shape[0]
    shape = jax.ShapeDtypeStruct((rows * 2 // 3 - 32, n * HD), F32)
    return call(
        functools.partial(spread_heads_kernel, n),
        (shape, shape, shape, jax.ShapeDtypeStruct((2, n * HD), F32)),
        scratch=[pltpu.VMEM((n, rows, 2 * HD), F32)],
        smem=1,
        n_in=1 + n,
    )(scal, *parts)


def pieces(size, count):
    step = size // count
    return [slice(i * step, (i + 1) * step) for i in range(count)]


def mean_of(values):
    return jnp.mean(values, axis=-1, keepdims=True)


def layer_stats(values):
    shifted = values - mean_of(values)
    inverse = lax.rsqrt(mean_of(shifted * shifted) + EPSILON)
    return (shifted * inverse, inverse)


def norm_back(grad_norm, normed, inverse, gain_row):
    scaled = grad_norm * gain_row
    return inverse * (scaled - mean_of(scaled) - normed * mean_of(scaled * normed))


def column_sum(values):
    return jnp.sum(values, axis=0, keepdims=True)


def first_norm_kernel(
    x_ref, pair_ref, far_ref, gain_ref, shift_ref, mid_ref, normed_ref, inverse_ref, low_ref
):
    branch = pair_ref[...].astype(F32) + far_ref[...].astype(F32) + shift_ref[0:1, :]
    normed, inverse = layer_stats(x_ref[...].astype(F32) + branch)
    middle = normed * gain_ref[0:1, :] + shift_ref[1:2, :]
    mid_ref[...] = middle
    normed_ref[...] = normed
    inverse_ref[...] = jnp.broadcast_to(inverse, inverse_ref.shape)
    low_ref[...] = middle.astype(BF16)


def first_norm(x, pair, far, gains, shift_rows):
    full = jax.ShapeDtypeStruct(x.shape, F32)
    return call(
        first_norm_kernel,
        (
            full,
            full,
            jax.ShapeDtypeStruct((x.shape[0], 128), F32),
            jax.ShapeDtypeStruct(x.shape, BF16),
        ),
        n_in=5,
    )(x, pair, far, gains, shift_rows)


def second_norm_kernel(
    mid_ref, pair_ref, far_ref, gain_ref, shift_ref, cot_ref, out_ref, grad_ref, low_ref, sum_ref
):
    mlp = pair_ref[...].astype(F32) + far_ref[...].astype(F32) + shift_ref[2:3, :]
    normed, inverse = layer_stats(mid_ref[...] + mlp)
    out_ref[...] = (normed * gain_ref[1:2, :] + shift_ref[3:4, :]).astype(BF16)
    cot = cot_ref[...].astype(F32)
    grad = norm_back(cot, normed, inverse, gain_ref[1:2, :])
    grad_ref[...] = grad
    low_ref[...] = grad.astype(BF16)
    sum_ref[0:1, :] = column_sum(cot * normed)
    sum_ref[1:2, :] = column_sum(grad)
    sum_ref[2:3, :] = column_sum(cot)


def second_norm(mid, pair, far, gains, shift_rows, cot):
    low = jax.ShapeDtypeStruct(mid.shape, BF16)
    return call(
        second_norm_kernel,
        (
            low,
            jax.ShapeDtypeStruct(mid.shape, F32),
            low,
            jax.ShapeDtypeStruct((3, mid.shape[1]), F32),
        ),
        n_in=6,
    )(mid, pair, far, gains, shift_rows, cot)


def first_back_kernel(
    two_ref, pair_ref, far_ref, normed_ref, inverse_ref, gain_ref, grad_ref, low_ref, sum_ref
):
    grad_mid = two_ref[...] + (pair_ref[...].astype(F32) + far_ref[...].astype(F32))
    normed = normed_ref[...]
    grad = norm_back(grad_mid, normed, inverse_ref[:, 0:1], gain_ref[0:1, :])
    grad_ref[...] = grad
    low_ref[...] = grad.astype(BF16)
    sum_ref[0:1, :] = column_sum(grad_mid * normed)
    sum_ref[1:2, :] = column_sum(grad)
    sum_ref[2:3, :] = column_sum(grad_mid)


def first_back(two, pair, far, normed, inverse, gains, after=()):
    return call(
        first_back_kernel,
        (
            jax.ShapeDtypeStruct(two.shape, F32),
            jax.ShapeDtypeStruct(two.shape, BF16),
            jax.ShapeDtypeStruct((3, two.shape[1]), F32),
        ),
        n_in=6,
        after=after,
    )(two, pair, far, normed, inverse, gains)


def last_sum_kernel(one_ref, pair_ref, far_ref, out_ref):
    total = pair_ref[...].astype(F32) + far_ref[...].astype(F32)
    out_ref[...] = (one_ref[...] + total).astype(BF16)


def row_cuts(refs):
    cuts = []
    start = 0
    for ref in refs:
        cuts.append((slice(start, start + ref.shape[0]), ref))
        start += ref.shape[0]
    return cuts


def column_groups(refs):
    groups = []
    column = 0
    for group in (refs[:1], refs[1:]):
        if group:
            width = group[0].shape[1]
            groups.append((slice(column, column + width), row_cuts(group)))
            column += width
    return groups


def sum_of(terms):
    total = terms[0]
    for term in terms[1:]:
        total = total + term
    return total


def feed_kernel(n_parts, *refs):
    own_ref, other_ref, bias_ref = refs[:3]
    ups = row_cuts(refs[3 : 3 + n_parts])
    downs = column_groups(refs[3 + n_parts : 3 + 2 * n_parts])
    pre_ref, act_ref, part_refs = refs[3 + 2 * n_parts], refs[4 + 2 * n_parts], refs[-2:]
    rows = own_ref.shape[0]
    for h, in_ref in enumerate((own_ref, other_ref)):
        pre = sum_of([mm(in_ref[:, cut], ref[...]) for cut, ref in ups]) + bias_ref[...]
        act = gelu_value(pre).astype(BF16)
        pre_ref[h * rows : (h + 1) * rows, :] = pre
        act_ref[h * rows : (h + 1) * rows, :] = act
        for columns, pieces in downs:
            part = sum_of([mm(act[:, cut], ref[...]) for cut, ref in pieces])
            part_refs[h][:, columns] = part.astype(BF16)


def feed(own, other, bias, ups, downs):
    rows, width = own.shape
    units = bias.shape[1]
    part = jax.ShapeDtypeStruct((rows, width), BF16)
    return call(
        functools.partial(feed_kernel, len(ups)),
        (
            jax.ShapeDtypeStruct((2 * rows, units), F32),
            jax.ShapeDtypeStruct((2 * rows, units), BF16),
            part,
            part,
        ),
        n_in=3 + 2 * len(ups),
    )(own, other, bias, *ups, *downs)


def feed_back_kernel(n_parts, *refs):
    own_ref, other_ref, pre_ref = refs[:3]
    ups = row_cuts(refs[3 : 3 + n_parts])
    downs = column_groups(refs[3 + n_parts : 3 + 2 * n_parts])
    low_ref, sum_ref, part_refs = refs[3 + 2 * n_parts], refs[4 + 2 * n_parts], refs[-2:]
    rows = own_ref.shape[0]
    sums = []
    for h, in_ref in enumerate((own_ref, other_ref)):
        terms = []
        for columns, pieces in downs:
            grads = [mm(in_ref[:, columns], ref[...], NT) for _, ref in pieces]
            terms.append(grads[0] if len(grads) == 1 else jnp.concatenate(grads, axis=1))
        grad = sum_of(terms)
        low = (grad * gelu_slope(pre_ref[h * rows : (h + 1) * rows, :])).astype(BF16)
        low_ref[h * rows : (h + 1) * rows, :] = low
        sums.append(column_sum(low.astype(F32)))
        for cut, ref in ups:
            part_refs[h][:, cut] = mm(low, ref[...], NT).astype(BF16)
    sum_ref[...] = sums[0] + sums[1]


def feed_back(own, other, pre, ups, downs, after=()):
    rows, width = own.shape
    units = pre.shape[1]
    part = jax.ShapeDtypeStruct((rows, width), BF16)
    return call(
        functools.partial(feed_back_kernel, len(ups)),
        (
            jax.ShapeDtypeStruct((2 * rows, units), BF16),
            jax.ShapeDtypeStruct((1, units), F32),
            part,
            part,
        ),
        n_in=3 + 2 * len(ups),
        after=after,
    )(own, other, pre, *ups, *downs)


def gelu_value(values):
    return 0.5 * values * (1.0 + lax.erf(values * 0.7071067811865476))


def gelu_slope(values):
    return (
        0.5 * (1.0 + lax.erf(values * 0.7071067811865476))
        + values * jnp.exp(-0.5 * values * values) * 0.3989422804014327
    )


def on_device(
    hidden, lengths, w_qkv, b_qkv, w_out, norm_gain, shifts, up_weight, b_up, down_weight, cotangent
):
    sequences, local_len, width = hidden.shape
    half = local_len // 2
    rows = sequences * local_len
    own_rows = rows // 2
    n_f = lax.axis_size("fsdp")
    part = width // n_f
    cols = w_qkv.shape[2]
    f_at = lax.axis_index("fsdp")
    core = lax.axis_index("tp") % 2

    def localise(value):
        value = turn(value, 2, f_at * part)
        value = turn(value, 1, core * half)
        return value

    x_slots = localise(hidden)
    x_rows = x_slots.reshape(rows, width)
    x_own = x_slots[:, :half].reshape(own_rows, width)
    cot_own = localise(cotangent)[:, :half].reshape(own_rows, width)

    w_parts = few(gather_parts(w_qkv.reshape(part, 3 * cols)), 0)
    norm_gain, shifts, b_qkv, b_up, w_out, ups, downs, _ = tie(
        norm_gain,
        shifts,
        b_qkv,
        b_up,
        w_out,
        split_rows(up_weight),
        split_rows(down_weight),
        x_own,
    )
    bias_len = b_qkv.shape[2]
    unit_len = b_up.shape[1]
    vectors = jnp.concatenate(
        [norm_gain.reshape(-1), shifts.reshape(-1), b_qkv.reshape(-1), b_up.reshape(-1)]
    ).reshape(1, -1)
    vectors = jnp.concatenate(gather_parts(vectors), axis=0)
    cuts = [2 * part, 6 * part, 6 * part + 2 * bias_len]
    gains = vectors[:, : cuts[0]].reshape(n_f, 2, part).transpose(1, 0, 2).reshape(2, width)
    shift_rows = vectors[:, cuts[0] : cuts[1]].reshape(n_f, 4, part).transpose(1, 0, 2)
    shift_rows = shift_rows.reshape(4, width).astype(F32)
    gains = gains.astype(F32)
    back = (n_f - f_at) % n_f
    b_pair = vectors[:, cuts[1] : cuts[2]].reshape(n_f, 2, bias_len).transpose(1, 0, 2)
    b_pair = turn(b_pair, 1, back).reshape(2, cols).astype(F32)
    up_bias = turn(vectors[:, cuts[2] :], 0, back).reshape(1, n_f * unit_len).astype(F32)
    w_out_parts = few(gather_parts(w_out), 1)
    up_pieces = split_gather(up_weight, ups, 0)
    down_pieces = split_gather(down_weight, downs, 1)

    scal = jnp.concatenate(
        [
            lengths,
            (core * half).astype(jnp.int32).reshape(1),
            lax.axis_index("ctx").astype(jnp.int32).reshape(1),
        ]
    )
    heads = rotate_out(project(scal, x_rows, b_pair, w_parts, local_len))
    *attn_parts, lse, qkv_all = attend(scal, heads, after=up_pieces[1:2])
    x_gather, _ = tie(x_own, lse)
    x_all_own = lax.all_gather(x_gather, "ctx", axis=0)
    x_all_other = swap_core(x_all_own)
    attn_rows, own, other = outproj(
        scal, rotate_back(attn_parts), w_out_parts, after=up_pieces[2:] + down_pieces[1:2]
    )

    pair = add(own, swap_core(other), after=down_pieces[2:])
    far = swap_y(pair)
    middle, normed_one, inverse_one, mid_own = first_norm(
        x_own, pair, far, gains, shift_rows
    )
    mid_other = swap_core(mid_own)
    pre_act, act_low, *partial = feed(mid_own, mid_other, up_bias, up_pieces, down_pieces)

    result_own, grad_two, two_own, two_sums = second_norm(
        middle, *tp_pair(*partial), gains, shift_rows, cot_own
    )
    two_other = swap_core(two_own)
    down_blocks = grad_blocks([act_low], [two_own, two_other], n_f, 1)
    pre_low, unit_sums, *partial = feed_back(
        two_own, two_other, pre_act, up_pieces, down_pieces, after=down_blocks[:1]
    )
    down_blocks = scatter_start(down_blocks)
    pair, far = tp_pair(*partial)
    up_blocks = grad_blocks([mid_own, mid_other], [pre_low], n_f, 0)

    grad_one, one_own, one_sums = first_back(
        grad_two, pair, far, normed_one, inverse_one, gains, after=up_blocks[:1]
    )
    up_blocks = scatter_start(up_blocks)
    one_other = swap_core(one_own)
    norm_sums = jnp.concatenate([one_sums, two_sums], axis=0)
    unit_sums = turn(unit_sums, 1, f_at * unit_len)
    grad_parts = grad_attn(scal, one_own, one_other, w_out_parts, local_len)

    grad_heads = rotate_out(grad_parts)
    down_sum = add(*down_blocks, after=grad_heads[1:])
    down_step = line_first(down_sum)
    head_grads = attend_back(
        scal, qkv_all, lse, grad_heads, after=[down_sum, x_all_other]
    )

    out_blocks = scatter_start(
        out_gradient(
            attn_rows, one_own, one_other, norm_sums, swap_core(norm_sums), unit_sums, n_f,
            after=head_grads[:1],
        )
    )
    head_rows = rotate_back(head_grads)
    rest = rest_sum(up_blocks, out_blocks, after=head_rows[1:])
    rest_step = line_first(rest)
    down_sum = line_add(down_sum, down_step, after=head_rows[1:])
    down_step = line_second(down_sum)

    next_rest = line_add(rest, rest_step, after=[down_step])
    down_sum = line_add(down_sum, down_step, after=[rest_step])
    rest, rest_step = next_rest, line_second(next_rest)
    down_step = line_third(down_sum)
    qkv_blocks = scatter_start(
        grad_project(scal, x_all_own, x_all_other, head_grads, n_f, after=[rest])
    )
    qkv_parts = rotate_all(add(*qkv_blocks))
    own, other = grad_token(scal, head_rows, w_parts, after=[rest])
    other = swap_core(other)

    rest = line_add(rest, rest_step, after=[down_step] + qkv_parts[1:])
    rest_step = line_third(rest)
    pair = add(own, other, after=[rest])
    far = swap_y(pair)
    grad_tokens = call(last_sum_kernel, jax.ShapeDtypeStruct(one_own.shape, BF16), n_in=3)(
        grad_one, pair, far
    )
    grad_q, grad_k, grad_v, grad_bias = spread_heads(scal, qkv_parts)
    grad_qkv = jnp.stack([grad_q, grad_k, grad_v], axis=1)
    grad_bias = lax.dynamic_slice_in_dim(grad_bias, f_at * bias_len, bias_len, axis=1)
    grad_bias = grad_bias.reshape(b_qkv.shape)

    grad_down = line_pick(down_sum, down_step).astype(F32)

    def restore(own):
        both = share_core(own).reshape(2, sequences, half, width)
        both = turn(both, 0, core).transpose(1, 0, 2, 3).reshape(sequences, local_len, width)
        return turn(both, 2, ((n_f - f_at) % n_f) * part)

    result = restore(result_own)
    grad_up, grad_out, grad_gain, grad_shift, grad_unit = rest_pick(
        scal, rest, rest_step, part, w_out.shape, after=[result, grad_qkv, grad_down]
    )
    return (
        result,
        restore(grad_tokens),
        grad_qkv,
        grad_bias,
        grad_out,
        grad_gain,
        grad_shift,
        grad_up,
        grad_unit.reshape(b_up.shape),
        grad_down,
    )


def solution(mesh):
    in_specs = (
        P("fsdp", "ctx", None),
        P("fsdp"),
        P("fsdp", None, "tp"),
        P(None, "tp", "fsdp"),
        P("tp", "fsdp"),
        P(None, "fsdp"),
        P(None, "fsdp"),
        P("fsdp", "tp"),
        P("tp", "fsdp"),
        P("tp", "fsdp"),
        P("fsdp", "ctx", None),
    )
    out_specs = (
        P("fsdp", "ctx", None),
        P("fsdp", "ctx", None),
        P("fsdp", None, "tp"),
        P(None, "tp", "fsdp"),
        P("tp", "fsdp"),
        P(None, "fsdp"),
        P(None, "fsdp"),
        P("fsdp", "tp"),
        P("tp", "fsdp"),
        P("tp", "fsdp"),
    )
    return jax.shard_map(
        on_device, mesh=mesh, in_specs=in_specs, out_specs=out_specs, check_vma=False
    )
```
